32 devices in a mesh: prow: 4 (over y, core), pcol: 8 (over z, x).
Axes of the slice: x: 2, y: 2, z: 4, core: 2. Of those that a mesh axis runs over, the one named last changes fastest.
Arguments:
- assembly: float32 [4, 256, 2, 128, 128], P('prow', 'pcol'), may hold values from -6 to 6
- slot_tile: int32 [4, 256], P('prow', 'pcol'), may hold values from 0 to 255, as said below
- pivots: int32 [2, 128], replicated, may hold values from 0 to 8191, as said below
- inverses: float32 [2, 2, 128, 128], replicated, may hold values from -0.046875 to 0.046875
Outputs:
- factored: float32 [2, 8192, 2048], P(None, 'prow', 'pcol')
The draws below stay inside these ranges and needn't reach their ends.
Inputs may be any that keep to these rules, and one draw needn't show every extreme that they name: `slot_tile`: row p lists tile ids t = i*16 + b, i the row tile among those of prow p and b the column tile; each of prow p's tiles appears in exactly one slot. A device's 32 slots hold at most 5 tiles whose column owner b % 8 is one index, and every device holds exactly 5 for some owner. `pivots`: entry j of panel k is either k*128 + j (no swap) or a row at or past 2*128; the rows named in one panel differ.
All inputs are finite; a program needn't handle non-finite values.
Results may differ from the reference program's by a relative error of at most 0.00013.
Values sent between devices are 32-bit elements; how exact they have to be, the bound alone decides.
No kernel may reach another device: no remote copies, remote signals or barrier semaphores. Data moves between devices by JAX's collectives and lax.ppermute only.
A program may use at most 128 MiB of HBM per device.

```python
import jax
import jax.numpy as jnp
import numpy as np
from jax import lax

NB = 128
CBLK = 2
RT_DEV = 16
GRID_ROWS = 4
GRID_COLS = 8
M = 8192
NC = 2048
NCB = 16
SLOTS_DEV = 32
CAP = 5


def count_table():
    mean_load = CAP - 1
    counts = [CAP, mean_load - 1]
    remaining = SLOTS_DEV - 2 * mean_load
    for owner in range(2, GRID_COLS):
        take = min(mean_load, max(remaining, 0))
        counts.append(take)
        remaining = remaining - take
    return np.array(counts, np.int32)


def draw_slot_tile(key, part):
    base = jnp.array(count_table())
    slots = jnp.arange(SLOTS_DEV, dtype=jnp.int32)

    def one_row(prow_index):
        row_key = jax.random.fold_in(key, prow_index)
        counts = base[jax.random.permutation(jax.random.fold_in(row_key, 1), GRID_COLS)]
        ends = jnp.cumsum(counts)
        offset = jnp.sum((slots[:, None] >= ends[None, :]).astype(jnp.int32), axis=1)

        def dest_order(dest):
            return jax.random.permutation(jax.random.fold_in(row_key, 100 + dest), SLOTS_DEV)
        orders = jax.vmap(dest_order)(jnp.arange(GRID_COLS, dtype=jnp.int32))

        def one_source(source):
            dest = (source + offset) % GRID_COLS
            owned = orders[dest, slots]
            tile_ids = owned // CBLK * NCB + owned % CBLK * GRID_COLS + dest
            shuffle = jax.random.permutation(jax.random.fold_in(row_key, 5000 + source), SLOTS_DEV)
            return tile_ids[shuffle]
        return jax.vmap(one_source)(jnp.arange(GRID_COLS, dtype=jnp.int32)).reshape(-1)
    return jax.vmap(one_row)(jnp.arange(GRID_ROWS, dtype=jnp.int32)).astype(jnp.int32)


def draw_pivots(key, part):

    def one_panel(panel):
        panel_key = jax.random.fold_in(key, 7 + panel)
        rows = jax.random.permutation(jax.random.fold_in(panel_key, 1), M - 2 * NB - 1)[:NB - 1] + 2 * NB
        rows = jnp.concatenate([rows.astype(jnp.int32), jnp.array([M - 1], jnp.int32)])
        order = jax.random.permutation(jax.random.fold_in(panel_key, 2), NB)
        rows = rows[order]
        stay = (jax.random.randint(jax.random.fold_in(panel_key, 3), (NB,), 0, 4) == 0) & (order != NB - 1)
        return jnp.where(stay, panel * NB + jnp.arange(NB, dtype=jnp.int32), rows)
    return jax.vmap(one_panel)(jnp.arange(2, dtype=jnp.int32)).astype(jnp.int32)


def block_levels(own_key, extent, pieces, low, top_value):
    def one(dim, shards_of):
        draws = jax.random.uniform(jax.random.fold_in(jax.random.fold_in(own_key, 6), dim), (shards_of,), jnp.float32, low / len(pieces), top_value / len(pieces))
        return jnp.repeat(jnp.exp(draws), extent[dim] // shards_of).reshape((-1,) + (1,) * (len(extent) - dim - 1))

    factor_of = one(*pieces[0])
    for cut in pieces[1:]:
        factor_of = factor_of * one(*cut)
    return factor_of


def normal_values(key, shape, width, reach, split=(), kind=jnp.bfloat16):
    factor_of = block_levels(key, shape, split, -0.22, 0.18) if split else 1.0
    values = jax.random.normal(key, shape, jnp.float32) * width * factor_of
    return jnp.minimum(jnp.maximum(values, -reach), reach).astype(kind)


def setup_inputs(seed: int = 0) -> dict:
    key_list = jax.random.split(jax.random.key(seed), 5)
    assembly = normal_values(key_list[0], (GRID_ROWS, GRID_COLS * SLOTS_DEV, 2, NB, NB), 1.0, 6.0, ((0, 4), (1, 8)), jnp.float32)
    slot_tile = draw_slot_tile(jax.random.fold_in(key_list[4], 71), 0)
    pivots = draw_pivots(jax.random.fold_in(key_list[4], 71), 0)
    inverses = normal_values(key_list[3], (2, 2, NB, NB), (NB * NB) ** -0.5, 0.046875, (), jnp.float32)
    return {"assembly": assembly, "slot_tile": slot_tile, "pivots": pivots, "inverses": inverses}


def complex_product(left, right):
    def dot(a, b):
        return jnp.matmul(a, b, precision=lax.Precision.HIGHEST)
    real = dot(left[0], right[0]) - dot(left[1], right[1])
    imag = dot(left[0], right[1]) + dot(left[1], right[0])
    return jnp.stack([real, imag])


def reference(assembly, slot_tile, pivots, inverses):
    stacked = []
    for prow_index in range(GRID_ROWS):
        holder = jnp.zeros((RT_DEV * NCB, 2, NB, NB), assembly.dtype)
        holder = holder.at[slot_tile[prow_index]].set(assembly[prow_index])
        stacked.append(holder.reshape(RT_DEV, NCB, 2, NB, NB))
    grid = jnp.stack(stacked)
    matrix = grid.transpose(3, 1, 0, 4, 2, 5).reshape(2, M, NC)
    for panel in range(2):
        start = panel * NB
        diag_rows = start + jnp.arange(NB, dtype=jnp.int32)
        chosen = pivots[panel]
        old_top = matrix[:, diag_rows, :]
        picked = matrix[:, chosen, :]
        matrix = matrix.at[:, chosen, :].set(old_top)
        matrix = matrix.at[:, diag_rows, :].set(picked)
        upper = matrix[:, start:start + NB, start + NB:]
        lower = complex_product(matrix[:, start + NB:, start:start + NB], inverses[panel])
        matrix = matrix.at[:, start + NB:, start:start + NB].set(lower)
        matrix = matrix.at[:, start + NB:, start + NB:].add(-complex_product(lower, upper))
    stored = matrix.reshape(2, RT_DEV, GRID_ROWS, NB, CBLK, GRID_COLS, NB)
    stored = stored.transpose(0, 2, 1, 3, 5, 4, 6).reshape(2, M, NC)
    return stored
```

```python
import functools

import jax
import jax.numpy as jnp
from jax import lax
from jax.experimental import pallas as pl
from jax.experimental.pallas import tpu as pltpu
from jax.sharding import PartitionSpec as P

CBLK = 2
LINES = 2
F32 = jnp.float32
BF16 = jnp.bfloat16
VMEM_LIMIT = 48 * 1024 * 1024

ANY = pl.BlockSpec(memory_space=pl.ANY)
SMEM = pl.BlockSpec(memory_space=pltpu.SMEM)
VMEM = pl.BlockSpec(memory_space=pltpu.VMEM)


def params():
    return pltpu.CompilerParams(vmem_limit_bytes=VMEM_LIMIT)


def list_slots(ids_ref, pos, cnt, slots, cols_n, base):
    for o in range(cols_n + 1):
        cnt[o] = 0
    pos[cols_n * (base + 1)] = 0

    def one(j, carry):
        owner = lax.rem(ids_ref[j], cols_n)
        r = cnt[owner]
        cnt[owner] = r + 1
        pos[owner * (base + 1) + r] = j

        @pl.when(r >= base)
        def _():
            e = cnt[cols_n]

            @pl.when(e == 0)
            def _():
                pos[cols_n * (base + 1)] = j

            cnt[cols_n] = e + 1

        return carry

    lax.fori_loop(0, slots, one, 0)


def copy_listed(moves, sems):
    for n, (cond, src, dst) in enumerate(moves):

        @pl.when(cond)
        def _(n=n, src=src, dst=dst):
            pltpu.make_async_copy(src, dst, sems.at[n]).start()

    for n, (cond, src, dst) in enumerate(moves):

        @pl.when(cond)
        def _(n=n, src=src, dst=dst):
            pltpu.make_async_copy(src, dst, sems.at[n]).wait()


def pack_streams(tiles, ids, me, cols_n, base):
    slots = tiles.shape[0]
    one = tiles.shape[1:]

    def kernel(ids_ref, me_ref, tiles_ref, mine_ref, other_ref, extra_ref, pos, cnt, sems):
        list_slots(ids_ref, pos, cnt, slots, cols_n, base)
        line = lax.rem(me_ref[0], LINES)
        moves = []
        for ref, owner in ((mine_ref, line), (other_ref, LINES - 1 - line)):
            for r in range(base):
                moves.append((r < cnt[owner], tiles_ref.at[pos[owner * (base + 1) + r]], ref.at[r]))
        moves.append((cnt[cols_n] > 0, tiles_ref.at[pos[cols_n * (base + 1)]], extra_ref.at[0]))
        copy_listed(moves, sems)

    return pl.pallas_call(
        kernel,
        out_shape=(
            jax.ShapeDtypeStruct((base,) + one, F32),
            jax.ShapeDtypeStruct((base,) + one, F32),
            jax.ShapeDtypeStruct((1,) + one, F32),
        ),
        in_specs=[SMEM, SMEM, ANY],
        out_specs=(ANY, ANY, ANY),
        scratch_shapes=[
            pltpu.SMEM((cols_n * (base + 1) + 1,), jnp.int32),
            pltpu.SMEM((cols_n + 1,), jnp.int32),
            pltpu.SemaphoreType.DMA((2 * base + 1,)),
        ],
        compiler_params=params(),
        name="pack_streams",
    )(ids, me, tiles)


def pack_shifts(tiles, ids, me, cols_n, base):
    slots = tiles.shape[0]
    one = tiles.shape[1:]

    def kernel(ids_ref, me_ref, tiles_ref, *rest):
        outs, (pos, cnt, sems) = rest[: cols_n - 1], rest[cols_n - 1 :]
        list_slots(ids_ref, pos, cnt, slots, cols_n, base)
        moves = []
        for k in range(1, cols_n):
            owner = lax.rem(me_ref[0] + k, cols_n)
            for r in range(base):
                moves.append(
                    (
                        (r < cnt[owner]) & (owner >= LINES),
                        tiles_ref.at[pos[owner * (base + 1) + r]],
                        outs[k - 1].at[r],
                    )
                )
        copy_listed(moves, sems)

    return pl.pallas_call(
        kernel,
        out_shape=tuple(jax.ShapeDtypeStruct((base,) + one, F32) for _ in range(1, cols_n)),
        in_specs=[SMEM, SMEM, ANY],
        out_specs=tuple(ANY for _ in range(1, cols_n)),
        scratch_shapes=[
            pltpu.SMEM((cols_n * (base + 1) + 1,), jnp.int32),
            pltpu.SMEM((cols_n + 1,), jnp.int32),
            pltpu.SemaphoreType.DMA(((cols_n - 1) * base,)),
        ],
        compiler_params=params(),
        name="pack_shifts",
    )(ids, me, tiles)


def place(parts, tables, outs_n, name):
    one = parts[0].shape[1:]
    counts = [p.shape[0] for p in parts]
    table = jnp.concatenate(tables)
    total = sum(counts)
    size = outs_n[1]
    n_out = outs_n[0]

    def kernel(table_ref, *rest):
        ins, outs, sems = rest[: len(parts)], rest[len(parts) : -1], rest[-1]
        moves = []
        at = 0
        for part, count in zip(ins, counts):
            for n in range(count):
                where = table_ref[at]
                for o in range(n_out):
                    inside = (where >= o * size) & (where < (o + 1) * size)
                    moves.append((inside, part.at[n], outs[o].at[where - o * size], at))
                at += 1
        for cond, src, dst, s in moves:

            @pl.when(cond)
            def _(src=src, dst=dst, s=s):
                pltpu.make_async_copy(src, dst, sems.at[s]).start()

        for cond, src, dst, s in moves:

            @pl.when(cond)
            def _(src=src, dst=dst, s=s):
                pltpu.make_async_copy(src, dst, sems.at[s]).wait()

    return pl.pallas_call(
        kernel,
        out_shape=tuple(jax.ShapeDtypeStruct((size,) + one, F32) for _ in range(n_out)),
        in_specs=[SMEM] + [ANY] * len(parts),
        out_specs=tuple(ANY for _ in range(n_out)),
        scratch_shapes=[pltpu.SemaphoreType.DMA((total,))],
        compiler_params=params(),
        name=name,
    )(table, *parts)


def extract(parts, tables, source_rows, tiles_n, name):
    block = parts[0].shape[-1]
    counts = [p.shape[0] for p in parts]
    table = jnp.concatenate(tables)
    total = sum(counts)
    picks = source_rows.shape[0]

    def kernel(table_ref, rows_ref, *rest):
        ins, (held, picked, sems) = rest[: len(parts)], rest[len(parts) :]
        moves = []
        at = 0
        for part, count in zip(ins, counts):
            for n in range(count):
                where = table_ref[at]
                moves.append((where >= 0, part.at[n], held.at[where]))
                at += 1
        for n, (cond, src, dst) in enumerate(moves):

            @pl.when(cond)
            def _(n=n, src=src, dst=dst):
                pltpu.make_async_copy(src, dst, sems.at[n]).start()

        picked[...] = jnp.zeros_like(picked)
        for n, (cond, src, dst) in enumerate(moves):

            @pl.when(cond)
            def _(n=n, src=src, dst=dst):
                pltpu.make_async_copy(src, dst, sems.at[n]).wait()

        def one(j, carry):
            row = rows_ref[j]

            @pl.when(row >= 0)
            def _():
                tile, inner = row // block, lax.rem(row, block)
                for m in range(CBLK):
                    for c in range(2):
                        picked[2 * m + c, pl.ds(j, 1), :] = held[
                            tile * CBLK + m, c, pl.ds(inner, 1), :
                        ]

            return carry

        lax.fori_loop(0, picks, one, 0)

    return pl.pallas_call(
        kernel,
        out_shape=(
            jax.ShapeDtypeStruct((tiles_n, 2, block, block), F32),
            jax.ShapeDtypeStruct((2 * CBLK, picks, block), F32),
        ),
        in_specs=[SMEM, SMEM] + [ANY] * len(parts),
        out_specs=(VMEM, VMEM),
        scratch_shapes=[pltpu.SemaphoreType.DMA((total,))],
        compiler_params=params(),
        name=name,
    )(table, source_rows, *parts)


def exchange(picked, top, my_row, rows_n):
    total = picked
    step = 1
    while step < rows_n:
        total = total + lax.ppermute(total, "prow", [(p, p ^ step) for p in range(rows_n)])
        step *= 2
    held = top
    step = 2
    while step < rows_n:
        got = lax.ppermute(held, "prow", [(p, p + step) for p in range(step)])
        held = jnp.where((my_row >= step) & (my_row < 2 * step), got, held)
        step *= 2
    other = lax.ppermute(held, "prow", [(p, p ^ 1) for p in range(rows_n)])
    even = my_row % 2 == 0
    old = jnp.stack([jnp.where(even, held, other), jnp.where(even, other, held)])
    return total, old


def replace_rows(targets_ref, old_ref, held, block, picks):
    def one(j, carry):
        row = targets_ref[j]

        @pl.when(row >= 0)
        def _():
            tile, inner = row // block, lax.rem(row, block)
            half, at = j // block, lax.rem(j, block)
            for m in range(CBLK):
                for c in range(2):
                    held[tile * CBLK + m, c, pl.ds(inner, 1), :] = old_ref[
                        half, m, c, pl.ds(at, 1), :
                    ]

        return carry

    lax.fori_loop(0, picks, one, 0)


def split(x):
    high = x.astype(BF16)
    return high, (x - high.astype(F32)).astype(BF16)


def dot3(x, w_high, w_low):
    high, low = split(x)
    return (
        jnp.dot(high, w_high, preferred_element_type=F32)
        + jnp.dot(high, w_low, preferred_element_type=F32)
        + jnp.dot(low, w_high, preferred_element_type=F32)
    )


def store_complex(high_ref, low_ref, row, col, re, im):
    k, n = re.shape
    for r, c, value in ((0, 0, re), (0, 1, im), (1, 0, -im), (1, 1, re)):
        high, low = split(value)
        rows, cols = pl.ds(row + r * k, k), pl.ds(col + c * n, n)
        high_ref[rows, cols] = high
        low_ref[rows, cols] = low


def panel_factors(held, new, old, inverses, targets, my_row):
    block = held.shape[-1]
    row_tiles = held.shape[0] // CBLK
    picks = targets.shape[0]

    def kernel(tgt, row_ref, held_in, new_ref, old_ref, inv_ref, out_ref, top_ref, held_ref, *w):
        held_ref[...] = held_in[...]
        replace_rows(tgt, old_ref, held_ref, block, picks)
        i0h, i0l, i1h, i1l, uh, ul = w
        store_complex(i0h, i0l, 0, 0, inv_ref[0, 0], inv_ref[0, 1])
        store_complex(i1h, i1l, 0, 0, inv_ref[1, 0], inv_ref[1, 1])
        store_complex(uh, ul, 0, 0, new_ref[2, :block], new_ref[3, :block])

        @pl.when(row_ref[0] == 1)
        def _():
            for m in range(CBLK):
                for c in range(2):
                    held_ref[m, c] = new_ref[2 * m + c, block:]

        lower = dot3(
            jnp.concatenate([new_ref[0, block:], new_ref[1, block:]], axis=1), i0h[...], i0l[...]
        )
        top_ref[0], top_ref[1] = lower[:, :block], lower[:, block:]

        def one(i, carry):
            x0 = jnp.concatenate([held_ref[i * CBLK, 0], held_ref[i * CBLK, 1]], axis=1)
            x1 = jnp.concatenate([held_ref[i * CBLK + 1, 0], held_ref[i * CBLK + 1, 1]], axis=1)
            l0 = dot3(x0, i0h[...], i0l[...])
            l1 = dot3(x1 - dot3(l0, uh[...], ul[...]), i1h[...], i1l[...])
            out_ref[i, 0], out_ref[i, 1] = l0[:, :block], l0[:, block:]
            out_ref[i, 2], out_ref[i, 3] = l1[:, :block], l1[:, block:]
            return carry

        lax.fori_loop(0, row_tiles, one, 0)

    wide = pltpu.VMEM((2 * block, 2 * block), BF16)
    return pl.pallas_call(
        kernel,
        out_shape=(
            jax.ShapeDtypeStruct((row_tiles, 4, block, block), F32),
            jax.ShapeDtypeStruct((2, block, block), F32),
        ),
        in_specs=[SMEM, SMEM, VMEM, VMEM, VMEM, VMEM],
        out_specs=(VMEM, VMEM),
        scratch_shapes=[pltpu.VMEM(held.shape, F32)] + [wide] * 6,
        compiler_params=params(),
        name="panel_factors",
    )(targets, my_row, held, new, old, inverses)


def update(held, new, old, lower, lower_top, targets, my_row, my_col, rows_n):
    block = held.shape[-1]
    row_tiles = held.shape[0] // CBLK
    picks = targets.shape[0]

    def kernel(tgt, row_ref, col_ref, held_in, new_ref, old_ref, low_ref, top_ref, out_ref, held_ref, wh, wl):
        held_ref[...] = held_in[...]
        replace_rows(tgt, old_ref, held_ref, block, picks)
        for m in range(CBLK):
            store_complex(wh, wl, 0, 2 * m * block, new_ref[2 * m, :block], new_ref[2 * m + 1, :block])
        top = jnp.concatenate([top_ref[0], top_ref[1]], axis=1)
        first = dot3(top, wh[: 2 * block, :], wl[: 2 * block, :])
        for m in range(CBLK):
            re = new_ref[2 * m, block:] - first[:, 2 * m * block : (2 * m + 1) * block]
            im = new_ref[2 * m + 1, block:] - first[:, (2 * m + 1) * block : (2 * m + 2) * block]
            store_complex(wh, wl, 2 * block, 2 * m * block, re, im)

            @pl.when(row_ref[0] == 1)
            def _(m=m, re=re, im=im):
                out_ref[0, :block, m * block : (m + 1) * block] = re
                out_ref[1, :block, m * block : (m + 1) * block] = im

            @pl.when(row_ref[0] == 0)
            def _(m=m):
                for c in range(2):
                    out_ref[c, :block, m * block : (m + 1) * block] = new_ref[2 * m + c, :block]

        def one(i, carry):
            row_tile = i * rows_n + row_ref[0]

            @pl.when(row_tile >= 2)
            def _():
                x = jnp.concatenate([low_ref[i, n] for n in range(4)], axis=1)
                y = dot3(x, wh[...], wl[...])
                rows = pl.ds(pl.multiple_of(i * block, block), block)
                for m in range(CBLK):
                    for c in range(2):
                        at = (2 * m + c) * block
                        out_ref[c, rows, m * block : (m + 1) * block] = (
                            held_ref[i * CBLK + m, c] - y[:, at : at + block]
                        )

            for panel in range(2):

                @pl.when((col_ref[0] == panel) & (row_tile > panel))
                def _(panel=panel):
                    rows = pl.ds(pl.multiple_of(i * block, block), block)
                    for c in range(2):
                        out_ref[c, rows, :block] = low_ref[i, 2 * panel + c]

            return carry

        lax.fori_loop(0, row_tiles, one, 0)

    return pl.pallas_call(
        kernel,
        out_shape=jax.ShapeDtypeStruct((2, row_tiles * block, CBLK * block), F32),
        in_specs=[SMEM] * 3 + [VMEM] * 5,
        out_specs=VMEM,
        scratch_shapes=[
            pltpu.VMEM(held.shape, F32),
            pltpu.VMEM((4 * block, 4 * block), BF16),
            pltpu.VMEM((4 * block, 4 * block), BF16),
        ],
        compiler_params=params(),
        name="update",
    )(targets, my_row, my_col, held, new, old, lower, lower_top)


def per_device(assembly, slot_tile, pivots, inverses):
    cols_n = lax.axis_size("pcol")
    rows_n = lax.axis_size("prow")
    my_col = lax.axis_index("pcol")
    my_row = lax.axis_index("prow")
    tiles = assembly[0]
    slots = tiles.shape[0]
    block = tiles.shape[-1]
    width = CBLK * cols_n
    row_tiles = slots // CBLK
    base = (slots + cols_n - 1) // cols_n
    excess_max = slots // (base + 1)
    depth = cols_n // LINES
    line, level = my_col % LINES, my_col // LINES
    me = my_col.astype(jnp.int32).reshape(1)
    me_row = my_row.astype(jnp.int32).reshape(1)
    ids = slot_tile[0]

    def shift(x, k, keep=lambda d: True):
        pairs = [(i, (i + k) % cols_n) for i in range(cols_n)]
        return lax.ppermute(x, "pcol", [(a, b) for a, b in pairs if keep(b)])

    def swap(x):
        return lax.ppermute(x, "pcol", [(i, i ^ 1) for i in range(cols_n)])

    def chain(x):
        ups, downs = [], []
        up = down = x
        for t in range(1, depth):
            up = lax.ppermute(
                up, "pcol", [(i, i + LINES) for i in range((t - 1) * LINES, cols_n - LINES)]
            )
            down = lax.ppermute(
                down, "pcol", [(i, i - LINES) for i in range(LINES, cols_n - (t - 1) * LINES)]
            )
            ups.append(up)
            downs.append(down)
        return ups, downs

    mine, other, extra = pack_streams(tiles, ids, me, cols_n, base)
    partner = swap(other)
    ups_m, downs_m = chain(mine)
    ups_e, downs_e = chain(extra)
    ups_p, downs_p = chain(partner)
    shifted = pack_shifts(tiles, ids, me, cols_n, base)
    arrived = [shift(shifted[k - 1], k, lambda d: d >= LINES) for k in range(1, cols_n)]

    near = [ids] + [shift(ids, k) for k in range(1, cols_n)]
    order = jnp.arange(cols_n, dtype=jnp.int32)
    sources = (my_col - order) % cols_n
    all_ids = jnp.stack(near)
    all_ids = jnp.sum(
        jnp.where(order[:, None, None] == sources[None, :, None], all_ids[None], 0), axis=1
    )
    owner = all_ids % cols_n
    slot_order = jnp.arange(slots, dtype=jnp.int32)
    earlier = slot_order[None, :] < slot_order[:, None]
    rank = jnp.sum(((owner[:, :, None] == owner[:, None, :]) & earlier[None]).astype(jnp.int32), axis=2)
    over = rank >= base
    over_rank = jnp.sum((over[:, None, :] & earlier[None]).astype(jnp.int32), axis=2)
    local_id = all_ids // width * CBLK + all_ids % width // cols_n
    most = jnp.max(jnp.sum(over.astype(jnp.int32), axis=1))
    step = 1
    most = jnp.broadcast_to(most, (8, 128))
    while step < rows_n:
        most = jnp.maximum(most, lax.ppermute(most, "prow", [(p, p ^ step) for p in range(rows_n)]))
        step *= 2

    def stream_table(stream):
        hit = (
            (owner[:, None, :] == stream)
            & ~over[:, None, :]
            & (rank[:, None, :] == jnp.arange(base, dtype=jnp.int32)[None, :, None])
        )
        return jnp.sum(jnp.where(hit, local_id[:, None, :] + 1, 0), axis=2) - 1

    def excess_table(stream):
        hit = (
            (owner[:, None, :] == stream)
            & over[:, None, :]
            & (over_rank[:, None, :] == jnp.arange(excess_max, dtype=jnp.int32)[None, :, None])
        )
        return jnp.sum(jnp.where(hit, local_id[:, None, :] + 1, 0), axis=2) - 1

    def at_source(table, source, valid):
        row = jnp.sum(jnp.where(order[:, None] == source, table, 0), axis=0)
        return jnp.where(valid, row, -1)

    line_extra = jnp.concatenate(ups_e[::-1] + [extra] + downs_e)
    line_extra = lax.dynamic_slice_in_dim(line_extra, depth - 1 - level, depth, axis=0)
    cross_extra = swap(line_extra)

    def gather_rest():
        def nth(e):
            hit = (order[:, None] == my_col) & over & (over_rank == e)
            return jnp.sum(jnp.where(hit, slot_order[None, :], 0))

        rest = jnp.stack([lax.dynamic_index_in_dim(tiles, nth(e), 0, False) for e in range(1, excess_max)])
        return lax.all_gather(rest, "pcol").reshape((-1,) + tiles.shape[1:])

    def no_rest():
        return jnp.zeros((cols_n * (excess_max - 1),) + tiles.shape[1:], F32)

    rest = lax.cond(most[0, 0] > 1, gather_rest, no_rest)

    def by_column(table):
        return jnp.where(table >= 0, table % CBLK * row_tiles + table // CBLK, -1)

    line_table = by_column(stream_table(line))
    line_over = by_column(excess_table(line))
    other_line = LINES - 1 - line
    parts, tables = [mine, partner], [
        at_source(line_table, my_col, True),
        at_source(line_table, level * LINES + other_line, True),
    ]
    for t in range(1, depth):
        for got, source_level in ((ups_m, level - t), (downs_m, level + t)):
            parts.append(got[t - 1])
            valid = (source_level >= 0) & (source_level < depth)
            tables.append(at_source(line_table, source_level * LINES + line, valid))
        for got, source_level in ((ups_p, level - t), (downs_p, level + t)):
            parts.append(got[t - 1])
            valid = (source_level >= 0) & (source_level < depth)
            tables.append(at_source(line_table, source_level * LINES + other_line, valid))
    levels = jnp.arange(depth, dtype=jnp.int32)

    def firsts(table, which):
        return jnp.sum(
            jnp.where(order[None, :] == (levels * LINES + which)[:, None], table[None, :, 0], 0), axis=1
        )

    parts += [line_extra, cross_extra, rest]
    tables += [firsts(line_over, line), firsts(line_over, other_line), line_over[:, 1:].reshape(-1)]
    panel_mine, column_rest = place(parts, tables, (CBLK, row_tiles), "place_streams")
    panel_other = swap(panel_mine)

    picks = jnp.arange(2 * block, dtype=jnp.int32)
    first, second = pivots[0], pivots[1]
    same = (second[:, None] == first[None, :]) & (first[None, :] >= 2 * block)
    chained = jnp.sum(jnp.where(same, picks[None, :block], 0), axis=1)
    second_source = jnp.where(jnp.any(same, axis=1), chained, second)
    wanted = jnp.concatenate([first, second_source])
    named = jnp.concatenate([first, second])

    def local_row(row, keep):
        ours = (row // block % rows_n == my_row) & keep
        return jnp.where(ours, row // block // rows_n * block + row % block, -1)

    source_rows = local_row(wanted, True)
    targets = local_row(named, named != picks)

    tile_order = jnp.arange(row_tiles, dtype=jnp.int32) * CBLK
    held_p, picked_p = extract(
        [panel_mine, panel_other], [tile_order + line, tile_order + other_line], source_rows, slots, "panel_rows"
    )
    new_p, old_p = exchange(picked_p, held_p[:CBLK], my_row, rows_n)
    lower, lower_top = panel_factors(held_p, new_p, old_p, inverses, targets, me_row)

    own_table, own_over = stream_table(my_col), excess_table(my_col)
    gathered = my_col < LINES
    here = (owner == my_col) & (order[:, None] == my_col)
    self_table = jnp.max(jnp.where(here, local_id, -1), axis=0)
    parts, tables = [tiles], [jnp.where(gathered, -1, self_table)]
    for k in range(1, cols_n):
        parts.append(arrived[k - 1])
        tables.append(at_source(own_table, (my_col - k) % cols_n, ~gathered))
    foreign = ~gathered & (order[:, None] != my_col)
    own_over = jnp.where(foreign, own_over, -1)
    parts += [line_extra, cross_extra, rest, panel_mine, column_rest]
    tables += [firsts(own_over, line), firsts(own_over, other_line), own_over[:, 1:].reshape(-1)]
    tables += [jnp.where(gathered, tile_order, -1), jnp.where(gathered, tile_order + 1, -1)]
    held, picked = extract(parts, tables, source_rows, slots, "own_rows")
    new, old = exchange(picked, held[:CBLK], my_row, rows_n)
    return update(held, new, old, lower, lower_top, targets, me_row, me, rows_n)


def solution(mesh):
    in_specs = (P("prow", "pcol", None, None, None), P("prow", "pcol"), P(), P())
    out_specs = P(None, "prow", "pcol")
    return jax.shard_map(
        per_device, mesh=mesh, in_specs=in_specs, out_specs=out_specs, check_vma=False
    )
```

```python
import jax
import jax.numpy as jnp
from jax import lax
from jax.experimental import pallas as pl
from jax.experimental.pallas import tpu as pltpu
from jax.sharding import PartitionSpec as P

CBLK = 2
LINES = 2
F32 = jnp.float32
BF16 = jnp.bfloat16
MIB = 1024 * 1024

ANY = pl.BlockSpec(memory_space=pl.ANY)
SMEM = pl.BlockSpec(memory_space=pltpu.SMEM)
VMEM = pl.BlockSpec(memory_space=pltpu.VMEM)


def call(kernel, mib, **kw):
    return pl.pallas_call(
        kernel,
        compiler_params=pltpu.CompilerParams(vmem_limit_bytes=mib * MIB),
        cost_estimate=pl.CostEstimate(flops=0, bytes_accessed=0, transcendentals=0),
        **kw,
    )


def list_slots(ids_ref, pos, cnt, slots, cols_n, base):
    for o in range(cols_n + 1):
        cnt[o] = 0
    pos[cols_n * (base + 1)] = 0

    def one(j, carry):
        owner = lax.rem(ids_ref[j], cols_n)
        r = cnt[owner]
        cnt[owner] = r + 1
        pos[owner * (base + 1) + r] = j

        @pl.when(r >= base)
        def _():
            e = cnt[cols_n]

            @pl.when(e == 0)
            def _():
                pos[cols_n * (base + 1)] = j

            cnt[cols_n] = e + 1

        return carry

    lax.fori_loop(0, slots, one, 0)


def copy_listed(moves, sems):
    for n, (cond, src, dst) in enumerate(moves):

        @pl.when(cond)
        def _(n=n, src=src, dst=dst):
            pltpu.make_async_copy(src, dst, sems.at[n]).start()

    for n, (cond, src, dst) in enumerate(moves):

        @pl.when(cond)
        def _(n=n, src=src, dst=dst):
            pltpu.make_async_copy(src, dst, sems.at[n]).wait()


def pack_streams(tiles, ids, cols_n, base):
    slots = tiles.shape[0]
    count = LINES * base + 1

    def kernel(ids_ref, tiles_ref, out_ref, pos, cnt, sems):
        list_slots(ids_ref, pos, cnt, slots, cols_n, base)
        moves = []
        for o in range(LINES):
            for r in range(base):
                moves.append((r < cnt[o], tiles_ref.at[pos[o * (base + 1) + r]], out_ref.at[o * base + r]))
        moves.append((cnt[cols_n] > 0, tiles_ref.at[pos[cols_n * (base + 1)]], out_ref.at[LINES * base]))
        copy_listed(moves, sems)

    return call(
        kernel,
        2,
        out_shape=jax.ShapeDtypeStruct((count,) + tiles.shape[1:], F32),
        in_specs=[SMEM, ANY],
        out_specs=ANY,
        scratch_shapes=[
            pltpu.SMEM((cols_n * (base + 1) + 1,), jnp.int32),
            pltpu.SMEM((cols_n + 1,), jnp.int32),
            pltpu.SemaphoreType.DMA((count,)),
        ],
        name="pack_streams",
    )(ids, tiles)


def pack_shifts(tiles, ids, me, cols_n, base):
    slots = tiles.shape[0]

    def kernel(ids_ref, me_ref, tiles_ref, *rest):
        outs, (pos, cnt, sems) = rest[: cols_n - 1], rest[cols_n - 1 :]
        list_slots(ids_ref, pos, cnt, slots, cols_n, base)
        moves = []
        for k in range(1, cols_n):
            owner = lax.rem(me_ref[0] + k, cols_n)
            for r in range(base):
                moves.append(
                    (
                        (r < cnt[owner]) & (owner >= LINES),
                        tiles_ref.at[pos[owner * (base + 1) + r]],
                        outs[k - 1].at[r],
                    )
                )
        copy_listed(moves, sems)

    return call(
        kernel,
        2,
        out_shape=tuple(jax.ShapeDtypeStruct((base,) + tiles.shape[1:], F32) for _ in range(1, cols_n)),
        in_specs=[SMEM, SMEM, ANY],
        out_specs=tuple(ANY for _ in range(1, cols_n)),
        scratch_shapes=[
            pltpu.SMEM((cols_n * (base + 1) + 1,), jnp.int32),
            pltpu.SMEM((cols_n + 1,), jnp.int32),
            pltpu.SemaphoreType.DMA(((cols_n - 1) * base,)),
        ],
        name="pack_shifts",
    )(ids, me, tiles)


def unwritten(shape):
    def kernel(out_ref):
        pass

    return call(kernel, 2, out_shape=jax.ShapeDtypeStruct(shape, F32), out_specs=ANY, name="unwritten")()


def extract(parts, tables, source_rows, odd, tiles_n, name):
    block = parts[0].shape[-1]
    bits = block.bit_length() - 1
    counts = [p.shape[0] for p in parts]
    table = jnp.concatenate(tables)
    wide = 2 * CBLK

    def kernel(table_ref, rows_ref, odd_ref, *rest):
        ins, (held, keep, send, top, sem) = rest[: len(parts)], rest[len(parts) :]
        at = 0
        for part, count in zip(ins, counts):
            for n in range(count):
                where = table_ref[at]

                @pl.when(where >= 0)
                def _(part=part, n=n, where=where):
                    pltpu.make_async_copy(part.at[n], held.at[where], sem).start()

                at += 1
        keep[...] = jnp.zeros_like(keep)
        send[...] = jnp.zeros_like(send)
        pltpu.make_async_copy(held, held, sem).wait()
        for m in range(CBLK):
            for c in range(2):
                top[2 * m + c] = held[m, c]
        for out, half in ((keep, odd_ref[0]), (send, 1 - odd_ref[0])):

            def one(j, carry, out=out, half=half):
                row = rows_ref[half * block + j]

                @pl.when(row >= 0)
                def _():
                    tile = lax.shift_right_logical(row, bits) * CBLK
                    inner = row & (block - 1)
                    for m in range(CBLK):
                        for c in range(2):
                            out[2 * m + c, pl.ds(j, 1), :] = held[tile + m, c, pl.ds(inner, 1), :]

                return carry

            lax.fori_loop(0, block, one, 0, unroll=4)

    part_rows = jax.ShapeDtypeStruct((wide, block, block), F32)
    return call(
        kernel,
        12,
        out_shape=(jax.ShapeDtypeStruct((tiles_n, 2, block, block), F32), part_rows, part_rows, part_rows),
        in_specs=[SMEM, SMEM, SMEM] + [ANY] * len(parts),
        out_specs=(VMEM, VMEM, VMEM, VMEM),
        scratch_shapes=[pltpu.SemaphoreType.DMA],
        name=name,
    )(table, source_rows, odd, *parts)


def exchange(keep, send, top, my_row, rows_n):
    def cross(x, step):
        return lax.ppermute(x, "prow", [(p, p ^ step) for p in range(rows_n)])

    held = top
    step = 2
    while step < rows_n:
        got = lax.ppermute(held, "prow", [(p, p + step) for p in range(step)])
        held = jnp.where((my_row >= step) & (my_row < 2 * step), got, held)
        step *= 2
    total = keep + cross(send, 1)
    step = 2
    while step < rows_n:
        total = total + cross(total, step)
        step *= 2
    return (total, cross(total, 1)), (held, cross(held, 1))


def replace_rows(targets_ref, odd, old_refs, held, block):
    bits = block.bit_length() - 1

    for ref, half in ((old_refs[0], odd), (old_refs[1], 1 - odd)):

        def one(j, carry, ref=ref, half=half):
            row = targets_ref[half * block + j]

            @pl.when(row >= 0)
            def _():
                tile = lax.shift_right_logical(row, bits) * CBLK
                inner = row & (block - 1)
                for m in range(CBLK):
                    for c in range(2):
                        held[tile + m, c, pl.ds(inner, 1), :] = ref[2 * m + c, pl.ds(j, 1), :]

            return carry

        lax.fori_loop(0, block, one, 0, unroll=4)


def split(x):
    high = x.astype(BF16)
    return high, (x - high.astype(F32)).astype(BF16)


def dot3(high, low, w_high, w_low):
    return (
        jnp.dot(high, w_high, preferred_element_type=F32)
        + jnp.dot(high, w_low, preferred_element_type=F32)
        + jnp.dot(low, w_high, preferred_element_type=F32)
    )


def store_complex(high_ref, low_ref, row, col, re, im):
    k, n = re.shape
    for r, c, value in ((0, 0, re), (0, 1, im), (1, 0, -im), (1, 1, re)):
        high, low = split(value)
        rows, cols = pl.ds(row + r * k, k), pl.ds(col + c * n, n)
        high_ref[rows, cols] = high
        low_ref[rows, cols] = low


def panel_factors(held, new, old, inverses, targets, my_row, group):
    block = held.shape[-1]
    row_tiles = held.shape[0] // CBLK
    rows = row_tiles * block

    def kernel(tgt, row_ref, held_in, new_a, new_b, old_a, old_b, inv_ref, high_ref, low_ref, top_ref, *rest):
        held_ref, new_ref, i0h, i0l, i1h, i1l, uh, ul, sem = rest
        odd = lax.rem(row_ref[0], 2)
        copy = pltpu.make_async_copy(held_in, held_ref, sem)
        copy.start()
        new_ref[odd] = new_a[...]
        new_ref[1 - odd] = new_b[...]
        store_complex(i0h, i0l, 0, 0, inv_ref[0, 0], inv_ref[0, 1])
        store_complex(i1h, i1l, 0, 0, inv_ref[1, 0], inv_ref[1, 1])
        store_complex(uh, ul, 0, 0, new_ref[0, 2], new_ref[0, 3])
        lower = dot3(
            *split(jnp.concatenate([new_ref[1, 0], new_ref[1, 1]], axis=1)), i0h[...], i0l[...]
        )
        top_ref[...] = lower
        copy.wait()
        replace_rows(tgt, odd, (old_a, old_b), held_ref, block)

        @pl.when(row_ref[0] == 1)
        def _():
            for m in range(CBLK):
                for c in range(2):
                    held_ref[m, c] = new_ref[1, 2 * m + c]

        def one(g, carry):
            x = [
                jnp.concatenate(
                    [
                        jnp.concatenate(
                            [held_ref[(g * group + t) * CBLK + m, 0], held_ref[(g * group + t) * CBLK + m, 1]], axis=1
                        )
                        for t in range(group)
                    ],
                    axis=0,
                )
                for m in range(CBLK)
            ]
            at = pl.ds(pl.multiple_of(g * (group * block), group * block), group * block)
            l0h, l0l = split(dot3(*split(x[0]), i0h[...], i0l[...]))
            high_ref[at, : 2 * block] = l0h
            low_ref[at, : 2 * block] = l0l
            y = x[1] - dot3(l0h, l0l, uh[...], ul[...])
            l1h, l1l = split(dot3(*split(y), i1h[...], i1l[...]))
            high_ref[at, 2 * block :] = l1h
            low_ref[at, 2 * block :] = l1l
            return carry

        lax.fori_loop(0, row_tiles // group, one, 0)

    wide = pltpu.VMEM((2 * block, 2 * block), BF16)
    return call(
        kernel,
        20,
        out_shape=(
            jax.ShapeDtypeStruct((rows, 4 * block), BF16),
            jax.ShapeDtypeStruct((rows, 4 * block), BF16),
            jax.ShapeDtypeStruct((block, 2 * block), F32),
        ),
        in_specs=[SMEM, SMEM, ANY] + [VMEM] * 5,
        out_specs=(VMEM, VMEM, VMEM),
        scratch_shapes=[pltpu.VMEM(held.shape, F32), pltpu.VMEM((2, 2 * CBLK, block, block), F32)]
        + [wide] * 6
        + [pltpu.SemaphoreType.DMA],
        name="panel_factors",
    )(targets, my_row, held, *new, *old, inverses)


def update(held, new, old, high, low, lower_top, targets, my_row, my_col, rows_n, group):
    block = held.shape[-1]
    row_tiles = held.shape[0] // CBLK
    rows = row_tiles * block
    steps = row_tiles // group
    span = group * block

    def kernel(tgt, row_ref, col_ref, held_in, new_a, new_b, old_a, old_b, high_in, low_in, top_ref, out_ref, *rest):
        held_ref, new_ref, high_ref, low_ref, res_ref, wh, wl, sem, in_sems, out_sems = rest
        odd = lax.rem(row_ref[0], 2)
        copies = [pltpu.make_async_copy(held_in, held_ref, sem)]
        copies[0].start()
        for g in range(steps):
            at = pl.ds(g * span, span)
            for n, (src, dst) in enumerate(((high_in, high_ref), (low_in, low_ref))):
                pltpu.make_async_copy(src.at[at], dst.at[at], in_sems.at[2 * g + n]).start()
        new_ref[odd] = new_a[...]
        new_ref[1 - odd] = new_b[...]
        for m in range(CBLK):
            store_complex(wh, wl, 0, 2 * m * block, new_ref[0, 2 * m], new_ref[0, 2 * m + 1])
        first = dot3(*split(top_ref[...]), wh[: 2 * block, :], wl[: 2 * block, :])
        second = []
        for n in range(2 * CBLK):
            second.append(new_ref[1, n] - first[:, n * block : (n + 1) * block])
            new_ref[1, n] = second[n]
        for m in range(CBLK):
            store_complex(wh, wl, 2 * block, 2 * m * block, second[2 * m], second[2 * m + 1])
        copies[0].wait()
        replace_rows(tgt, odd, (old_a, old_b), held_ref, block)
        for g in range(steps):
            at = pl.ds(g * span, span)
            for n, (src, dst) in enumerate(((high_in, high_ref), (low_in, low_ref))):
                pltpu.make_async_copy(src.at[at], dst.at[at], in_sems.at[2 * g + n]).wait()
            y = dot3(high_ref[at, :], low_ref[at, :], wh[...], wl[...])
            for t in range(group):
                tile = g * group + t
                for m in range(CBLK):
                    for c in range(2):
                        n = 2 * m + c
                        res_ref[c, tile * block : (tile + 1) * block, m * block : (m + 1) * block] = (
                            held_ref[tile * CBLK + m, c]
                            - y[t * block : (t + 1) * block, n * block : (n + 1) * block]
                        )
            for panel in range(2):

                @pl.when(col_ref[0] == panel)
                def _(panel=panel, at=at):
                    for c in range(2):
                        cols = slice((2 * panel + c) * block, (2 * panel + c + 1) * block)
                        res_ref[c, at, :block] = high_ref[at, cols].astype(F32) + low_ref[at, cols].astype(F32)

            if g == 0:
                for p in range(2):

                    @pl.when(row_ref[0] == p)
                    def _(p=p):
                        for c in range(2):
                            for m in range(CBLK):
                                res_ref[c, :block, m * block : (m + 1) * block] = new_ref[p, 2 * m + c]

                @pl.when((row_ref[0] == 1) & (col_ref[0] == 0))
                def _():
                    for c in range(2):
                        res_ref[c, :block, :block] = top_ref[:, c * block : (c + 1) * block]

            for c in range(2):
                pltpu.make_async_copy(res_ref.at[c, at], out_ref.at[c, at], out_sems.at[2 * g + c]).start()
        for g in range(steps):
            at = pl.ds(g * span, span)
            for c in range(2):
                pltpu.make_async_copy(res_ref.at[c, at], out_ref.at[c, at], out_sems.at[2 * g + c]).wait()

    return call(
        kernel,
        24,
        out_shape=jax.ShapeDtypeStruct((2, rows, CBLK * block), F32),
        in_specs=[SMEM] * 3 + [ANY] + [VMEM] * 4 + [ANY] * 2 + [VMEM],
        out_specs=ANY,
        scratch_shapes=[
            pltpu.VMEM(held.shape, F32),
            pltpu.VMEM((2, 2 * CBLK, block, block), F32),
            pltpu.VMEM((rows, 4 * block), BF16),
            pltpu.VMEM((rows, 4 * block), BF16),
            pltpu.VMEM((2, rows, CBLK * block), F32),
            pltpu.VMEM((4 * block, 4 * block), BF16),
            pltpu.VMEM((4 * block, 4 * block), BF16),
            pltpu.SemaphoreType.DMA,
            pltpu.SemaphoreType.DMA((2 * steps,)),
            pltpu.SemaphoreType.DMA((2 * steps,)),
        ],
        name="update",
    )(targets, my_row, my_col, held, *new, *old, high, low, lower_top)


def per_device(assembly, slot_tile, pivots, inverses):
    cols_n = lax.axis_size("pcol")
    rows_n = lax.axis_size("prow")
    my_col = lax.axis_index("pcol")
    my_row = lax.axis_index("prow")
    tiles = assembly[0]
    slots = tiles.shape[0]
    block = tiles.shape[-1]
    width = CBLK * cols_n
    row_tiles = slots // CBLK
    base = (slots + cols_n - 1) // cols_n
    excess_max = slots // (base + 1)
    depth = cols_n // LINES
    group = 4 if row_tiles % 4 == 0 else 1
    line, level = my_col % LINES, my_col // LINES
    me = my_col.astype(jnp.int32).reshape(1)
    me_row = my_row.astype(jnp.int32).reshape(1)
    odd = me_row % 2
    ids = slot_tile[0]

    def swap(x, low=0, high=depth):
        return lax.ppermute(x, "pcol", [(i, i ^ 1) for i in range(low * LINES, high * LINES)])

    packed = pack_streams(tiles, ids, cols_n, base)
    parts, sources = [packed, swap(packed)], [(level, line), (level, 1 - line)]
    up = down = packed
    for t in range(1, depth):
        up = lax.ppermute(up, "pcol", [(i, i + LINES) for i in range((t - 1) * LINES, cols_n - LINES)])
        down = lax.ppermute(down, "pcol", [(i, i - LINES) for i in range(LINES, cols_n - (t - 1) * LINES)])
        parts += [up, down, swap(up, t, depth), swap(down, 0, depth - t)]
        sources += [(level - t, line), (level + t, line), (level - t, 1 - line), (level + t, 1 - line)]

    shifted = pack_shifts(tiles, ids, me, cols_n, base)
    arrived = []
    for k in range(1, cols_n):
        pairs = [(i, (i + k) % cols_n) for i in range(cols_n)]
        arrived.append(lax.ppermute(shifted[k - 1], "pcol", [(a, b) for a, b in pairs if b >= LINES]))

    near = lax.optimization_barrier((ids, packed))[0][None]
    step = 1
    while step < cols_n:
        near = jnp.concatenate([near, lax.ppermute(near, "pcol", [(i, i ^ step) for i in range(cols_n)])])
        step *= 2
    order = jnp.arange(cols_n, dtype=jnp.int32)
    all_ids = jnp.sum(
        jnp.where((order[:, None] == (order[None, :] ^ my_col))[:, :, None], near[:, None, :], 0), axis=0
    )
    owner = all_ids % cols_n
    slot_order = jnp.arange(slots, dtype=jnp.int32)
    earlier = slot_order[None, :] < slot_order[:, None]
    rank = jnp.sum(((owner[:, :, None] == owner[:, None, :]) & earlier[None]).astype(jnp.int32), axis=2)
    over = rank >= base
    over_rank = jnp.sum((over[:, None, :] & earlier[None]).astype(jnp.int32), axis=2)
    most = jnp.broadcast_to(jnp.max(jnp.sum(over.astype(jnp.int32), axis=1)), (8, 128))
    step = 1
    while step < rows_n:
        most = jnp.maximum(most, lax.ppermute(most, "prow", [(p, p ^ step) for p in range(rows_n)]))
        step *= 2

    def ids_where(hit):
        return jnp.sum(jnp.where(hit, all_ids[:, None, :] + 1, 0), axis=2) - 1

    ranks = jnp.arange(base, dtype=jnp.int32)[None, :, None]
    over_ranks = jnp.arange(excess_max, dtype=jnp.int32)[None, :, None]

    def ranked(stream):
        return ids_where((owner[:, None, :] == stream) & ~over[:, None, :] & (rank[:, None, :] == ranks))

    excess = ids_where(over[:, None, :] & (over_rank[:, None, :] == over_ranks))
    sent = jnp.concatenate([ranked(o) for o in range(LINES)] + [excess[:, :1]], axis=1)
    later = excess[:, 1:].reshape(-1)

    def panel_place(t):
        return jnp.where((t >= 0) & (t % width < LINES), t // width * CBLK + t % width, -1)

    def own_place(t):
        return jnp.where((t >= 0) & (t % cols_n == my_col), t // width * CBLK + t % width // cols_n, -1)

    def by_part(table):
        source = jnp.stack([jnp.where((a >= 0) & (a < depth), a * LINES + b, -1) for a, b in sources])
        hit = source[:, None, None] == order[None, :, None]
        return (jnp.sum(jnp.where(hit, table[None] + 1, 0), axis=1) - 1).reshape(-1)

    def gather_rest():
        def nth(e):
            hit = (order[:, None] == my_col) & over & (over_rank == e)
            return jnp.sum(jnp.where(hit, slot_order[None, :], 0))

        rest = jnp.stack([lax.dynamic_index_in_dim(tiles, nth(e), 0, False) for e in range(1, excess_max)])
        return lax.all_gather(rest, "pcol").reshape((-1,) + tiles.shape[1:])

    def no_rest():
        return unwritten((cols_n * (excess_max - 1),) + tiles.shape[1:])

    rest = lax.cond(most[0, 0] > 1, gather_rest, no_rest)

    picks = jnp.arange(2 * block, dtype=jnp.int32)
    first, second = pivots[0], pivots[1]
    same = (second[:, None] == first[None, :]) & (first[None, :] >= 2 * block)
    chained = jnp.sum(jnp.where(same, picks[None, :block], 0), axis=1)
    second_source = jnp.where(jnp.any(same, axis=1), chained, second)
    replaced = jnp.any(same, axis=0)
    wanted = jnp.concatenate([first, second_source])
    named = jnp.concatenate([first, second])
    moved = (named != picks) & ~jnp.concatenate([replaced, jnp.zeros_like(replaced)])

    def local_row(row, keep):
        ours = (row // block % rows_n == my_row) & keep
        return jnp.where(ours, row // block // rows_n * block + row % block, -1)

    source_rows = local_row(wanted, True)
    targets = local_row(named, moved)

    tables = [by_part(panel_place(sent)), panel_place(later)]
    held_p, keep_p, send_p, top_p = extract(parts + [rest], tables, source_rows, odd, slots, "panel_rows")
    new_p, old_p = exchange(keep_p, send_p, top_p, my_row, rows_n)
    high, low, lower_top = panel_factors(held_p, new_p, old_p, inverses, targets, me_row, group)

    gathered = my_col < LINES
    mine = order[:, None] == my_col
    here = jnp.max(jnp.where(mine, own_place(all_ids), -1), axis=0)
    tables = [jnp.where(gathered, -1, here)]
    own_sent = own_place(ranked(my_col))
    for k in range(1, cols_n):
        row = jnp.sum(jnp.where(order[:, None] == (my_col - k) % cols_n, own_sent, 0), axis=0)
        tables.append(jnp.where(gathered, -1, row))
    use = gathered | ~mine
    tables += [by_part(jnp.where(use, own_place(sent), -1))]
    tables += [jnp.where(jnp.repeat(use[:, 0], excess_max - 1), own_place(later), -1)]
    held, keep, send, top = extract(
        [tiles] + arrived + parts + [rest], tables, source_rows, odd, slots, "own_rows"
    )
    new, old = exchange(keep, send, top, my_row, rows_n)
    return update(held, new, old, high, low, lower_top, targets, me_row, me, rows_n, group)


def solution(mesh):
    in_specs = (P("prow", "pcol", None, None, None), P("prow", "pcol"), P(), P())
    out_specs = P(None, "prow", "pcol")
    return jax.shard_map(
        per_device, mesh=mesh, in_specs=in_specs, out_specs=out_specs, check_vma=False
    )
```

```python
import functools

import jax
import jax.numpy as jnp
from jax import lax
from jax.experimental import pallas as pl
from jax.experimental.pallas import tpu as pltpu
from jax.sharding import PartitionSpec as P

CBLK = 2
LINES = 2
F32 = jnp.float32
BF16 = jnp.bfloat16
MIB = 1024 * 1024
META = 128

ANY = pl.BlockSpec(memory_space=pl.ANY)
SMEM = pl.BlockSpec(memory_space=pltpu.SMEM)
VMEM = pl.BlockSpec(memory_space=pltpu.VMEM)
HBM = pl.BlockSpec(memory_space=pltpu.HBM)


def call(kernel, mib, **kw):
    return pl.pallas_call(
        kernel,
        compiler_params=pltpu.CompilerParams(vmem_limit_bytes=mib * MIB),
        cost_estimate=pl.CostEstimate(flops=0, bytes_accessed=0, transcendentals=0),
        **kw,
    )


def list_slots(ids_ref, pos, meta, slots, cols_n, base, excess_max):
    first = cols_n * base
    for n in range(first + excess_max):
        meta[n] = -1
        pos[n] = 0
    for o in range(cols_n + 1):
        pos[first + excess_max + o] = 0

    def one(j, carry):
        t = ids_ref[j]
        owner = t & (cols_n - 1)
        r = pos[first + excess_max + owner]
        pos[first + excess_max + owner] = r + 1
        e = pos[first + excess_max + cols_n]
        over = (r >= base).astype(jnp.int32)
        pos[first + excess_max + cols_n] = e + over
        at = jnp.where(r >= base, first + e, owner * base + r)
        pos[at] = j
        meta[at] = t
        return carry

    lax.fori_loop(0, slots, one, 0)
    meta[first + excess_max] = pos[first + excess_max + cols_n]


def pack(tiles, ids, me, cols_n, base, excess_max):
    slots = tiles.shape[0]
    count = LINES * base + 1
    first = cols_n * base

    def kernel(ids_ref, me_ref, tiles_ref, stream_ref, *rest):
        outs, (meta, held, pos, sems) = rest[: cols_n - 1], rest[cols_n - 1 :]
        list_slots(ids_ref, pos, meta, slots, cols_n, base, excess_max)
        moves = []
        for n in range(count):
            at = n if n < LINES * base else first
            moves.append((meta[at] >= 0, pos[at], stream_ref.at[n]))
        for k in range(1, cols_n):
            owner = me_ref[0] ^ k
            for r in range(base):
                at = owner * base + r
                moves.append(((meta[at] >= 0) & (owner >= LINES), pos[at], outs[k - 1].at[r]))
        for n, (cond, slot, _) in enumerate(moves):

            @pl.when(cond)
            def _(n=n, slot=slot):
                pltpu.make_async_copy(tiles_ref.at[slot], held.at[n], sems.at[0, n]).start()

        for n, (cond, slot, dst) in enumerate(moves):

            @pl.when(cond)
            def _(n=n, slot=slot, dst=dst):
                pltpu.make_async_copy(tiles_ref.at[slot], held.at[n], sems.at[0, n]).wait()
                pltpu.make_async_copy(held.at[n], dst, sems.at[1, n]).start()

        for n, (cond, _, dst) in enumerate(moves):

            @pl.when(cond)
            def _(n=n, dst=dst):
                pltpu.make_async_copy(held.at[n], dst, sems.at[1, n]).wait()

    one = tiles.shape[1:]
    total = count + (cols_n - 1) * base
    got = call(
        kernel,
        8,
        out_shape=(pltpu.HBM((count,) + one, F32),)
        + tuple(pltpu.HBM((base,) + one, F32) for _ in range(1, cols_n))
        + (jax.ShapeDtypeStruct((META,), jnp.int32),),
        in_specs=[SMEM, SMEM, HBM],
        out_specs=tuple(HBM for _ in range(cols_n)) + (SMEM,),
        scratch_shapes=[
            pltpu.VMEM((total,) + one, F32),
            pltpu.SMEM((first + excess_max + cols_n + 1,), jnp.int32),
            pltpu.SemaphoreType.DMA((2, total)),
        ],
        name="pack",
    )(ids, me, tiles)
    return got[0], got[1:-1], got[-1]


def unwritten(shape):
    def kernel(out_ref):
        pass

    return call(kernel, 2, out_shape=jax.ShapeDtypeStruct(shape, F32), out_specs=HBM, name="unwritten")()


def extract(
    parts, origins, rest, near, ids, source_rows, me, odd, cols_n, base, tiles=None, arrived=(), arrived_from=()
):
    block = rest.shape[-1]
    bits = block.bit_length() - 1
    width = CBLK * cols_n
    width_bits, cols_bits = width.bit_length() - 1, cols_n.bit_length() - 1
    wide = 2 * CBLK
    own = tiles is not None
    count = LINES * base + 1
    depth = cols_n // LINES
    tiles_n = ids.shape[0]
    first = cols_n * base
    per = rest.shape[0] // cols_n

    def kernel(near_ref, ids_ref, rows_ref, me_ref, odd_ref, *rest_refs):
        part_refs, rest_refs = rest_refs[: len(parts)], rest_refs[len(parts) :]
        rest_ref, rest_refs = rest_refs[0], rest_refs[1:]
        if own:
            tiles_ref, arrived_refs = rest_refs[0], rest_refs[1 : 1 + len(arrived)]
        held_out, keep, send, top, held, sem, out_sem = rest_refs[-7:]
        me = me_ref[0]
        level, line = lax.shift_right_logical(me, 1), me & 1
        gathered = me < LINES

        def fetch(src, t, wanted):
            column = t & (width - 1)
            row = lax.shift_right_logical(t, width_bits)
            if own:
                ours = (column & (cols_n - 1)) == me
                place = row * CBLK + lax.shift_right_logical(column, cols_bits)
            else:
                ours = column < LINES
                place = row * CBLK + column

            @pl.when((t >= 0) & ours & wanted)
            def _():
                pltpu.make_async_copy(src, held.at[place], sem).start()

        if own:

            @pl.when(~gathered)
            def _():
                def one(j, carry):
                    fetch(tiles_ref.at[j], ids_ref[j], True)
                    return carry

                lax.fori_loop(0, tiles_n, one, 0)
                for ref, (k, pairs) in zip(arrived_refs, arrived_from):
                    here = functools.reduce(jnp.logical_or, [me == b for _, b in pairs])
                    for r in range(base):
                        fetch(ref.at[r], near_ref[k, me * base + r], here)

        for ref, (step, cross) in zip(part_refs, origins):
            if isinstance(step, tuple):
                by_level = step[0]
                for z in range(1, depth):
                    by_level = jnp.where(level == z, step[z], by_level)
                step = by_level
            at = level + step
            valid = (at >= 0) & (at < depth)
            source = at * LINES + (1 - line if cross else line)
            if own:
                valid = valid & (gathered | (source != me))

            @pl.when(valid)
            def _(ref=ref, source=source):
                k = source ^ me

                def streams():
                    for q in range(count - 1):
                        fetch(ref.at[q], near_ref[k, q], True)

                if own:
                    pl.when(gathered)(streams)
                else:
                    streams()
                fetch(ref.at[count - 1], near_ref[k, first], True)

        most = near_ref[0, first + per + 1]
        for k in range(1, cols_n):
            most = jnp.maximum(most, near_ref[k, first + per + 1])

        @pl.when(most > 1)
        def _():
            for k in range(cols_n):

                def one(e, carry, k=k):
                    fetch(rest_ref.at[k * per + e], near_ref[k, first + 1 + e], (gathered | (k > 0)) if own else True)
                    return carry

                lax.fori_loop(0, per, one, 0)

        pltpu.make_async_copy(held, held, sem).wait()
        copy_out = pltpu.make_async_copy(held, held_out, out_sem)
        copy_out.start()
        for m in range(CBLK):
            for c in range(2):
                top[2 * m + c] = held[m, c]
        for out, half in ((keep, odd_ref[0]), (send, 1 - odd_ref[0])):

            def pick(j, carry, out=out, half=half):
                row = rows_ref[half * block + j]
                here = row >= 0
                row = jnp.maximum(row, 0)
                tile = lax.shift_right_logical(row, bits) * CBLK
                inner = row & (block - 1)
                for m in range(CBLK):
                    for c in range(2):
                        value = held[tile + m, c, pl.ds(inner, 1), :]
                        out[2 * m + c, pl.ds(j, 1), :] = jnp.where(here, value, 0.0)
                return carry

            lax.fori_loop(0, block, pick, 0, unroll=8)
        copy_out.wait()

    part_rows = jax.ShapeDtypeStruct((wide, block, block), F32)
    operands = list(parts) + [rest] + ([tiles] + list(arrived) if own else [])
    operands = [pltpu.with_memory_space_constraint(x, pltpu.HBM) for x in operands]
    return call(
        kernel,
        12,
        out_shape=(pltpu.HBM((tiles_n, 2, block, block), F32), part_rows, part_rows, part_rows),
        in_specs=[SMEM] * 5 + [HBM] * len(operands),
        out_specs=(HBM, VMEM, VMEM, VMEM),
        scratch_shapes=[
            pltpu.VMEM((tiles_n, 2, block, block), F32),
            pltpu.SemaphoreType.DMA,
            pltpu.SemaphoreType.DMA,
        ],
        name="own_rows" if own else "panel_rows",
    )(near, ids, source_rows, me, odd, *operands)


def exchange(keep, send, top, my_row, rows_n):
    def cross(x, step):
        return lax.ppermute(x, "prow", [(p, p ^ step) for p in range(rows_n)])

    held = top
    step = 2
    while step < rows_n:
        got = lax.ppermute(held, "prow", [(p, p + step) for p in range(step)])
        held = jnp.where((my_row >= step) & (my_row < 2 * step), got, held)
        step *= 2
    total = keep + cross(send, 1)
    step = 2
    while step < rows_n:
        total = total + cross(total, step)
        step *= 2
    return (total, cross(total, 1)), (held, cross(held, 1))


def replace_rows(targets_ref, odd, old_refs, held, block):
    bits = block.bit_length() - 1

    spare = held.shape[0] - CBLK
    for ref, half in ((old_refs[0], odd), (old_refs[1], 1 - odd)):

        def one(j, carry, ref=ref, half=half):
            row = targets_ref[half * block + j]
            tile = jnp.where(row >= 0, lax.shift_right_logical(row, bits) * CBLK, spare)
            inner = row & (block - 1)
            for m in range(CBLK):
                for c in range(2):
                    held[tile + m, c, pl.ds(inner, 1), :] = ref[2 * m + c, pl.ds(j, 1), :]
            return carry

        lax.fori_loop(0, block, one, 0, unroll=8)


def split(x):
    high = x.astype(BF16)
    return high, (x - high.astype(F32)).astype(BF16)


def dot3(high, low, w_high, w_low):
    return (
        jnp.dot(high, w_high, preferred_element_type=F32)
        + jnp.dot(high, w_low, preferred_element_type=F32)
        + jnp.dot(low, w_high, preferred_element_type=F32)
    )


def store_complex(high_ref, low_ref, row, col, re, im):
    k, n = re.shape
    for r, c, value in ((0, 0, re), (0, 1, im), (1, 0, -im), (1, 1, re)):
        high, low = split(value)
        rows, cols = pl.ds(row + r * k, k), pl.ds(col + c * n, n)
        high_ref[rows, cols] = high
        low_ref[rows, cols] = low


def panel_factors(held, new, old, inverses, targets, my_row, group):
    block = held.shape[-1]
    row_tiles = held.shape[0] // CBLK
    rows = row_tiles * block

    def kernel(tgt, row_ref, held_in, new_a, new_b, old_a, old_b, inv_ref, high_ref, low_ref, top_ref, *rest):
        held_ref, new_ref, i0h, i0l, i1h, i1l, uh, ul, sem = rest
        odd = lax.rem(row_ref[0], 2)
        copy = pltpu.make_async_copy(held_in, held_ref.at[: CBLK * row_tiles], sem)
        copy.start()
        new_ref[odd] = new_a[...]
        new_ref[1 - odd] = new_b[...]
        store_complex(i0h, i0l, 0, 0, inv_ref[0, 0], inv_ref[0, 1])
        store_complex(i1h, i1l, 0, 0, inv_ref[1, 0], inv_ref[1, 1])
        store_complex(uh, ul, 0, 0, new_ref[0, 2], new_ref[0, 3])
        lower = dot3(
            *split(jnp.concatenate([new_ref[1, 0], new_ref[1, 1]], axis=1)), i0h[...], i0l[...]
        )
        top_ref[...] = lower
        copy.wait()
        replace_rows(tgt, odd, (old_a, old_b), held_ref, block)

        @pl.when(row_ref[0] == 1)
        def _():
            for m in range(CBLK):
                for c in range(2):
                    held_ref[m, c] = new_ref[1, 2 * m + c]

        def one(g, carry):
            x = [
                jnp.concatenate(
                    [
                        jnp.concatenate(
                            [held_ref[(g * group + t) * CBLK + m, 0], held_ref[(g * group + t) * CBLK + m, 1]], axis=1
                        )
                        for t in range(group)
                    ],
                    axis=0,
                )
                for m in range(CBLK)
            ]
            at = pl.ds(pl.multiple_of(g * (group * block), group * block), group * block)
            l0h, l0l = split(dot3(*split(x[0]), i0h[...], i0l[...]))
            high_ref[at, : 2 * block] = l0h
            low_ref[at, : 2 * block] = l0l
            y = x[1] - dot3(l0h, l0l, uh[...], ul[...])
            l1h, l1l = split(dot3(*split(y), i1h[...], i1l[...]))
            high_ref[at, 2 * block :] = l1h
            low_ref[at, 2 * block :] = l1l
            return carry

        lax.fori_loop(0, row_tiles // group, one, 0)

    wide = pltpu.VMEM((2 * block, 2 * block), BF16)
    return call(
        kernel,
        20,
        out_shape=(
            jax.ShapeDtypeStruct((rows, 4 * block), BF16),
            jax.ShapeDtypeStruct((rows, 4 * block), BF16),
            jax.ShapeDtypeStruct((block, 2 * block), F32),
        ),
        in_specs=[SMEM, SMEM, ANY] + [VMEM] * 5,
        out_specs=(VMEM, VMEM, VMEM),
        scratch_shapes=[pltpu.VMEM((held.shape[0] + CBLK,) + held.shape[1:], F32), pltpu.VMEM((2, 2 * CBLK, block, block), F32)]
        + [wide] * 6
        + [pltpu.SemaphoreType.DMA],
        name="panel_factors",
    )(targets, my_row, held, *new, *old, inverses)


def update(held, new, old, high, low, lower_top, targets, my_row, my_col, rows_n, group):
    block = held.shape[-1]
    row_tiles = held.shape[0] // CBLK
    rows = row_tiles * block
    steps = row_tiles // group
    span = group * block

    def kernel(tgt, row_ref, col_ref, held_in, new_a, new_b, old_a, old_b, high_in, low_in, top_ref, out_ref, *rest):
        held_ref, new_ref, high_ref, low_ref, res_ref, wh, wl, sem, in_sems, out_sems = rest
        odd = lax.rem(row_ref[0], 2)
        copy = pltpu.make_async_copy(held_in, held_ref.at[: CBLK * row_tiles], sem)
        copy.start()
        for g in range(steps):
            at = pl.ds(g * span, span)
            for n, (src, dst) in enumerate(((high_in, high_ref), (low_in, low_ref))):
                pltpu.make_async_copy(src.at[at], dst.at[at], in_sems.at[2 * g + n]).start()
        new_ref[odd] = new_a[...]
        new_ref[1 - odd] = new_b[...]
        for m in range(CBLK):
            store_complex(wh, wl, 0, 2 * m * block, new_ref[0, 2 * m], new_ref[0, 2 * m + 1])
        first = dot3(*split(top_ref[...]), wh[: 2 * block, :], wl[: 2 * block, :])
        second = []
        for n in range(2 * CBLK):
            second.append(new_ref[1, n] - first[:, n * block : (n + 1) * block])
            new_ref[1, n] = second[n]
        for m in range(CBLK):
            store_complex(wh, wl, 2 * block, 2 * m * block, second[2 * m], second[2 * m + 1])
        copy.wait()
        replace_rows(tgt, odd, (old_a, old_b), held_ref, block)
        for g in range(steps):
            at = pl.ds(g * span, span)
            for n, (src, dst) in enumerate(((high_in, high_ref), (low_in, low_ref))):
                pltpu.make_async_copy(src.at[at], dst.at[at], in_sems.at[2 * g + n]).wait()
            y = dot3(high_ref[at, :], low_ref[at, :], wh[...], wl[...])
            for t in range(group):
                tile = g * group + t
                for m in range(CBLK):
                    for c in range(2):
                        n = 2 * m + c
                        res_ref[c, tile * block : (tile + 1) * block, m * block : (m + 1) * block] = (
                            held_ref[tile * CBLK + m, c]
                            - y[t * block : (t + 1) * block, n * block : (n + 1) * block]
                        )
            for panel in range(2):

                @pl.when(col_ref[0] == panel)
                def _(panel=panel, at=at):
                    for c in range(2):
                        cols = slice((2 * panel + c) * block, (2 * panel + c + 1) * block)
                        res_ref[c, at, :block] = high_ref[at, cols].astype(F32) + low_ref[at, cols].astype(F32)

            if g == 0:
                for p in range(2):

                    @pl.when(row_ref[0] == p)
                    def _(p=p):
                        for c in range(2):
                            for m in range(CBLK):
                                res_ref[c, :block, m * block : (m + 1) * block] = new_ref[p, 2 * m + c]

                @pl.when((row_ref[0] == 1) & (col_ref[0] == 0))
                def _():
                    for c in range(2):
                        res_ref[c, :block, :block] = top_ref[:, c * block : (c + 1) * block]

            for c in range(2):
                pltpu.make_async_copy(res_ref.at[c, at], out_ref.at[c, at], out_sems.at[2 * g + c]).start()
        for g in range(steps):
            at = pl.ds(g * span, span)
            for c in range(2):
                pltpu.make_async_copy(res_ref.at[c, at], out_ref.at[c, at], out_sems.at[2 * g + c]).wait()

    return call(
        kernel,
        24,
        out_shape=jax.ShapeDtypeStruct((2, rows, CBLK * block), F32),
        in_specs=[SMEM] * 3 + [ANY] + [VMEM] * 4 + [ANY] * 2 + [VMEM],
        out_specs=ANY,
        scratch_shapes=[
            pltpu.VMEM((held.shape[0] + CBLK,) + held.shape[1:], F32),
            pltpu.VMEM((2, 2 * CBLK, block, block), F32),
            pltpu.VMEM((rows, 4 * block), BF16),
            pltpu.VMEM((rows, 4 * block), BF16),
            pltpu.VMEM((2, rows, CBLK * block), F32),
            pltpu.VMEM((4 * block, 4 * block), BF16),
            pltpu.VMEM((4 * block, 4 * block), BF16),
            pltpu.SemaphoreType.DMA,
            pltpu.SemaphoreType.DMA((2 * steps,)),
            pltpu.SemaphoreType.DMA((2 * steps,)),
        ],
        name="update",
    )(targets, my_row, my_col, held, *new, *old, high, low, lower_top)


def per_device(assembly, slot_tile, pivots, inverses):
    cols_n = lax.axis_size("pcol")
    rows_n = lax.axis_size("prow")
    my_col = lax.axis_index("pcol")
    my_row = lax.axis_index("prow")
    tiles = assembly[0]
    slots = tiles.shape[0]
    block = tiles.shape[-1]
    row_tiles = slots // CBLK
    base = (slots + cols_n - 1) // cols_n
    excess_max = slots // (base + 1)
    depth = cols_n // LINES
    group = 4 if row_tiles % 4 == 0 else 1
    level = my_col // LINES
    me = my_col.astype(jnp.int32).reshape(1)
    me_row = my_row.astype(jnp.int32).reshape(1)
    odd = me_row % 2
    ids = slot_tile[0]

    picks = jnp.arange(2 * block, dtype=jnp.int32)
    first, second = pivots[0], pivots[1]
    same = (second[:, None] == first[None, :]) & (first[None, :] >= 2 * block)
    chained = jnp.sum(jnp.where(same, picks[None, :block], 0), axis=1)
    second_source = jnp.where(jnp.any(same, axis=1), chained, second)
    replaced = jnp.any(same, axis=0)
    wanted = jnp.concatenate([first, second_source])
    named = jnp.concatenate([first, second])
    moved = (named != picks) & ~jnp.concatenate([replaced, jnp.zeros_like(replaced)])

    def local_row(row, keep):
        ours = (row // block % rows_n == my_row) & keep
        return jnp.where(ours, row // block // rows_n * block + row % block, -1)

    source_rows = local_row(wanted, True)
    targets = local_row(named, moved)

    def after(values, earlier):
        return lax.optimization_barrier((tuple(values), tuple(earlier)))[0]

    def swapped(phase):
        due = []
        for z in range(depth):
            chunks = []
            for t in range(1, depth):
                chunks += [("up", t)] * (z - t >= 0) + [("down", t)] * (z + t < depth)
            due.append(chunks[phase - 2])
        return due

    def shift_pairs(k, phase):
        zm, dx = k // LINES, k % LINES
        pairs = []
        for i in range(cols_n):
            due = depth + 1
            if dx == 0 and zm >= 2:
                due = depth if (i ^ k) // LINES == depth - 1 else depth - 1
            elif (dx == 1 and zm == depth // 2) or (dx == 0 and zm == 1):
                due = depth
            if (i ^ k) >= LINES and due == phase:
                pairs.append((i, i ^ k))
        return pairs

    packed, shifted, meta = pack(tiles, ids, me, cols_n, base, excess_max)
    parts, origins = [packed], [(0, False)]
    chunk = {("up", 0): packed, ("down", 0): packed}
    arrived, arrived_from = [], []
    done = []
    near = meta[None]
    for phase in range(1, depth + 2):
        work = []
        if phase < depth:
            t = phase
            up = [(i, i + LINES) for i in range((t - 1) * LINES, cols_n - LINES)]
            down = [(i, i - LINES) for i in range(LINES, cols_n - (t - 1) * LINES)]
            work.append((chunk["up", t - 1], up, ("up", t), (-t, False)))
            work.append((chunk["down", t - 1], down, ("down", t), (t, False)))
        if phase == 1:
            work.append((packed, [(i, i ^ 1) for i in range(cols_n)], None, (0, True)))
        elif phase <= depth:
            due = swapped(phase)
            x = chunk[due[0]]
            for key in sorted(set(due[1:]) - {due[0]}):
                here = functools.reduce(jnp.logical_or, [level == z for z in range(depth) if due[z] == key])
                x = jnp.where(here, chunk[key], x)
            steps = tuple(-t if d == "up" else t for d, t in due)
            work.append((x, [(i, i ^ 1) for i in range(cols_n)], None, (steps, True)))
        else:
            gathered_all = done
        for k in range(1, cols_n):
            pairs = shift_pairs(k, phase)
            if pairs:
                work.append((shifted[k - 1], pairs, k, pairs))
        before = done
        values = after([w[0] for w in work], done) if done else [w[0] for w in work]
        done = [lax.ppermute(x, "pcol", w[1]) for x, w in zip(values, work)]
        for got, (_, _, key, origin) in zip(done, work):
            if isinstance(key, int):
                arrived.append(got)
                arrived_from.append((key, origin))
            else:
                parts.append(got)
                origins.append(origin)
                if key is not None:
                    chunk[key] = got
        step = 1 << (phase - 1)
        if step < cols_n:
            if phase > 1:
                near = after([near], before)[0]
            got = lax.ppermute(near, "pcol", [(i, i ^ step) for i in range(cols_n)])
            near = jnp.concatenate([near, got])
            done = done + [near]
        if phase == 1:
            done = done + [source_rows, targets]
    shifted_all = done
    most = jnp.max(near[:, cols_n * base + excess_max])

    def gather_rest():
        mine = meta[cols_n * base + 1 : cols_n * base + excess_max]
        slot = jnp.sum(
            jnp.where(mine[:, None] == ids[None, :], jnp.arange(slots, dtype=jnp.int32)[None, :], 0), axis=1
        )
        rest = jnp.stack(
            [lax.dynamic_index_in_dim(tiles, slot[e], 0, False) for e in range(excess_max - 1)]
        )
        others = [
            lax.ppermute(rest, "pcol", [(i, i ^ k) for i in range(cols_n)]) for k in range(1, cols_n)
        ]
        return jnp.concatenate([rest] + others)

    def no_rest():
        return unwritten((cols_n * (excess_max - 1),) + tiles.shape[1:])

    rest = lax.cond(most > 1, gather_rest, no_rest)

    late_rows = after([source_rows], gathered_all)[0]
    held_p, keep_p, send_p, top_p = extract(
        parts, origins, rest, near, ids, late_rows, me, odd, cols_n, base
    )
    keep_p, send_p, top_p = after((keep_p, send_p, top_p), shifted_all)
    new_p, old_p = exchange(keep_p, send_p, top_p, my_row, rows_n)
    high, low, lower_top = panel_factors(held_p, new_p, old_p, inverses, targets, me_row, group)

    held, keep, send, top = extract(
        parts, origins, rest, near, ids, source_rows, me, odd, cols_n, base, tiles, arrived, arrived_from
    )
    new, old = exchange(keep, send, top, my_row, rows_n)
    return update(held, new, old, high, low, lower_top, targets, me_row, me, rows_n, group)


def solution(mesh):
    in_specs = (P("prow", "pcol", None, None, None), P("prow", "pcol"), P(), P())
    out_specs = P(None, "prow", "pcol")
    return jax.shard_map(
        per_device, mesh=mesh, in_specs=in_specs, out_specs=out_specs, check_vma=False
    )
```

```python
import functools

import jax
import jax.numpy as jnp
from jax import lax
from jax.experimental import pallas as pl
from jax.experimental.pallas import tpu as pltpu
from jax.sharding import PartitionSpec as P

CBLK = 2
LINES = 2
F32 = jnp.float32
BF16 = jnp.bfloat16
MIB = 1024 * 1024
META = 128

ANY = pl.BlockSpec(memory_space=pl.ANY)
SMEM = pl.BlockSpec(memory_space=pltpu.SMEM)
VMEM = pl.BlockSpec(memory_space=pltpu.VMEM)
HBM = pl.BlockSpec(memory_space=pltpu.HBM)


def call(kernel, mib, **kw):
    return pl.pallas_call(
        kernel,
        compiler_params=pltpu.CompilerParams(vmem_limit_bytes=mib * MIB),
        cost_estimate=pl.CostEstimate(flops=0, bytes_accessed=0, transcendentals=0),
        **kw,
    )


def list_slots(ids_ref, pos, meta, slots, cols_n, base, excess_max):
    first = cols_n * base
    for n in range(first + excess_max):
        meta[n] = -1
        pos[n] = 0
    for o in range(cols_n + 1):
        pos[first + excess_max + o] = 0

    def one(j, carry):
        t = ids_ref[j]
        owner = t & (cols_n - 1)
        r = pos[first + excess_max + owner]
        pos[first + excess_max + owner] = r + 1
        e = pos[first + excess_max + cols_n]
        over = (r >= base).astype(jnp.int32)
        pos[first + excess_max + cols_n] = e + over
        at = jnp.where(r >= base, first + e, owner * base + r)
        pos[at] = j
        meta[at] = t
        return carry

    lax.fori_loop(0, slots, one, 0)
    meta[first + excess_max] = pos[first + excess_max + cols_n]


def pack(tiles, ids, me, cols_n, base, excess_max):
    slots = tiles.shape[0]
    count = LINES * base + 1
    first = cols_n * base

    def kernel(ids_ref, me_ref, tiles_ref, stream_ref, *rest):
        outs, (meta, held, pos, sems) = rest[: cols_n - 1], rest[cols_n - 1 :]
        list_slots(ids_ref, pos, meta, slots, cols_n, base, excess_max)
        moves = []
        for n in range(count):
            at = n if n < LINES * base else first
            moves.append((meta[at] >= 0, pos[at], stream_ref.at[n]))
        for k in range(1, cols_n):
            owner = me_ref[0] ^ k
            for r in range(base):
                at = owner * base + r
                moves.append(((meta[at] >= 0) & (owner >= LINES), pos[at], outs[k - 1].at[r]))
        for n, (cond, slot, _) in enumerate(moves):

            @pl.when(cond)
            def _(n=n, slot=slot):
                pltpu.make_async_copy(tiles_ref.at[slot], held.at[n], sems.at[0, n]).start()

        for n, (cond, slot, dst) in enumerate(moves):

            @pl.when(cond)
            def _(n=n, slot=slot, dst=dst):
                pltpu.make_async_copy(tiles_ref.at[slot], held.at[n], sems.at[0, n]).wait()
                pltpu.make_async_copy(held.at[n], dst, sems.at[1, n]).start()

        for n, (cond, _, dst) in enumerate(moves):

            @pl.when(cond)
            def _(n=n, dst=dst):
                pltpu.make_async_copy(held.at[n], dst, sems.at[1, n]).wait()

    one = tiles.shape[1:]
    total = count + (cols_n - 1) * base
    got = call(
        kernel,
        8,
        out_shape=(pltpu.HBM((count,) + one, F32),)
        + tuple(pltpu.HBM((base,) + one, F32) for _ in range(1, cols_n))
        + (jax.ShapeDtypeStruct((META,), jnp.int32),),
        in_specs=[SMEM, SMEM, HBM],
        out_specs=tuple(HBM for _ in range(cols_n)) + (SMEM,),
        scratch_shapes=[
            pltpu.VMEM((total,) + one, F32),
            pltpu.SMEM((first + excess_max + cols_n + 1,), jnp.int32),
            pltpu.SemaphoreType.DMA((2, total)),
        ],
        name="pack",
    )(ids, me, tiles)
    return got[0], got[1:-1], got[-1]


def unwritten(shape):
    def kernel(out_ref):
        pass

    return call(kernel, 2, out_shape=jax.ShapeDtypeStruct(shape, F32), out_specs=HBM, name="unwritten")()


def extract(
    parts, origins, rest, near, ids, source_rows, me, odd, cols_n, base, tiles=None, arrived=(), arrived_from=()
):
    block = rest.shape[-1]
    bits = block.bit_length() - 1
    width = CBLK * cols_n
    width_bits, cols_bits = width.bit_length() - 1, cols_n.bit_length() - 1
    wide = 2 * CBLK
    own = tiles is not None
    count = LINES * base + 1
    depth = cols_n // LINES
    tiles_n = ids.shape[0]
    first = cols_n * base
    per = rest.shape[0] // cols_n

    def kernel(near_ref, ids_ref, rows_ref, me_ref, odd_ref, *rest_refs):
        part_refs, rest_refs = rest_refs[: len(parts)], rest_refs[len(parts) :]
        rest_ref, rest_refs = rest_refs[0], rest_refs[1:]
        if own:
            tiles_ref, arrived_refs = rest_refs[0], rest_refs[1 : 1 + len(arrived)]
        held_out, keep, send, top, held, sem, out_sem = rest_refs[-7:]
        me = me_ref[0]
        level, line = lax.shift_right_logical(me, 1), me & 1
        gathered = me < LINES

        def fetch(src, t, wanted):
            column = t & (width - 1)
            row = lax.shift_right_logical(t, width_bits)
            if own:
                ours = (column & (cols_n - 1)) == me
                place = row * CBLK + lax.shift_right_logical(column, cols_bits)
            else:
                ours = column < LINES
                place = row * CBLK + column

            @pl.when((t >= 0) & ours & wanted)
            def _():
                pltpu.make_async_copy(src, held.at[place], sem).start()

        if own:

            @pl.when(~gathered)
            def _():
                def one(j, carry):
                    fetch(tiles_ref.at[j], ids_ref[j], True)
                    return carry

                lax.fori_loop(0, tiles_n, one, 0)
                for ref, (k, pairs) in zip(arrived_refs, arrived_from):
                    here = functools.reduce(jnp.logical_or, [me == b for _, b in pairs])
                    for r in range(base):
                        fetch(ref.at[r], near_ref[k, me * base + r], here)

        for ref, (step, cross) in zip(part_refs, origins):
            if isinstance(step, tuple):
                by_level = step[0]
                for z in range(1, depth):
                    by_level = jnp.where(level == z, step[z], by_level)
                step = by_level
            at = level + step
            valid = (at >= 0) & (at < depth)
            source = at * LINES + (1 - line if cross else line)
            if own:
                valid = valid & (gathered | (source != me))

            @pl.when(valid)
            def _(ref=ref, source=source):
                k = source ^ me

                def streams():
                    for q in range(count - 1):
                        fetch(ref.at[q], near_ref[k, q], True)

                if own:
                    pl.when(gathered)(streams)
                else:
                    streams()
                fetch(ref.at[count - 1], near_ref[k, first], True)

        most = near_ref[0, first + per + 1]
        for k in range(1, cols_n):
            most = jnp.maximum(most, near_ref[k, first + per + 1])

        @pl.when(most > 1)
        def _():
            for k in range(cols_n):

                def one(e, carry, k=k):
                    fetch(rest_ref.at[k * per + e], near_ref[k, first + 1 + e], (gathered | (k > 0)) if own else True)
                    return carry

                lax.fori_loop(0, per, one, 0)

        pltpu.make_async_copy(held, held, sem).wait()
        copy_out = pltpu.make_async_copy(held, held_out, out_sem)
        copy_out.start()
        for m in range(CBLK):
            for c in range(2):
                top[2 * m + c] = held[m, c]
        for out, half in ((keep, odd_ref[0]), (send, 1 - odd_ref[0])):

            def pick(j, carry, out=out, half=half):
                row = rows_ref[half * block + j]
                here = row >= 0
                row = jnp.maximum(row, 0)
                tile = lax.shift_right_logical(row, bits) * CBLK
                inner = row & (block - 1)
                for m in range(CBLK):
                    for c in range(2):
                        value = held[tile + m, c, pl.ds(inner, 1), :]
                        out[2 * m + c, pl.ds(j, 1), :] = jnp.where(here, value, 0.0)
                return carry

            lax.fori_loop(0, block, pick, 0, unroll=8)
        copy_out.wait()

    part_rows = jax.ShapeDtypeStruct((wide, block, block), F32)
    operands = list(parts) + [rest] + ([tiles] + list(arrived) if own else [])
    operands = [pltpu.with_memory_space_constraint(x, pltpu.HBM) for x in operands]
    return call(
        kernel,
        12,
        out_shape=(pltpu.HBM((tiles_n, 2, block, block), F32), part_rows, part_rows, part_rows),
        in_specs=[SMEM] * 5 + [HBM] * len(operands),
        out_specs=(HBM, VMEM, VMEM, VMEM),
        scratch_shapes=[
            pltpu.VMEM((tiles_n, 2, block, block), F32),
            pltpu.SemaphoreType.DMA,
            pltpu.SemaphoreType.DMA,
        ],
        name="own_rows" if own else "panel_rows",
    )(near, ids, source_rows, me, odd, *operands)


def exchange(keep, send, top, far, my_row, rows_n, earlier=(), meanwhile=None):
    def cross(x, step):
        return lax.ppermute(x, "prow", [(p, p ^ step) for p in range(rows_n)])

    total = keep + cross(send, 1)
    if rows_n == 4:
        there = far[None, :, None]
        second = my_row >= 2
        message = jnp.where(there & ~second, top, total)
        message = lax.optimization_barrier((message, tuple(earlier)))[0]
        got = cross(message, 2)
        if meanwhile is not None:
            got = lax.optimization_barrier((got, meanwhile))[0]
        total = total + jnp.where(there & second, 0.0, got)
        held = jnp.where(second, got, top)
        return (total, cross(total, 1)), (held, cross(held, 1)), got
    held = top
    step = 2
    while step < rows_n:
        got = lax.ppermute(held, "prow", [(p, p + step) for p in range(step)])
        held = jnp.where((my_row >= step) & (my_row < 2 * step), got, held)
        total = total + cross(total, step)
        step *= 2
    return (total, cross(total, 1)), (held, cross(held, 1)), total


def fix_chained(chain_ref, new_ref, odd, old_refs, block):
    @pl.when(chain_ref[block] > 0)
    def _():
        def one(i, carry):
            j = chain_ref[i]

            @pl.when((j >= 0) & (odd == 0))
            def _():
                new_ref[1, :, pl.ds(i, 1), :] = old_refs[0][:, pl.ds(j, 1), :]

            @pl.when((j >= 0) & (odd == 1))
            def _():
                new_ref[1, :, pl.ds(i, 1), :] = old_refs[1][:, pl.ds(j, 1), :]

            return carry

        lax.fori_loop(0, block, one, 0)


def replace_rows(targets_ref, odd, old_refs, held, block):
    bits = block.bit_length() - 1

    spare = held.shape[0] - CBLK
    for ref, half in ((old_refs[0], odd), (old_refs[1], 1 - odd)):

        def one(j, carry, ref=ref, half=half):
            row = targets_ref[half * block + j]
            tile = jnp.where(row >= 0, lax.shift_right_logical(row, bits) * CBLK, spare)
            inner = row & (block - 1)
            for m in range(CBLK):
                for c in range(2):
                    held[tile + m, c, pl.ds(inner, 1), :] = ref[2 * m + c, pl.ds(j, 1), :]
            return carry

        lax.fori_loop(0, block, one, 0, unroll=8)


def split(x):
    high = x.astype(BF16)
    return high, (x - high.astype(F32)).astype(BF16)


def dot3(high, low, w_high, w_low):
    return (
        jnp.dot(high, w_high, preferred_element_type=F32)
        + jnp.dot(high, w_low, preferred_element_type=F32)
        + jnp.dot(low, w_high, preferred_element_type=F32)
    )


def store_complex(high_ref, low_ref, row, col, re, im):
    k, n = re.shape
    for r, c, value in ((0, 0, re), (0, 1, im), (1, 0, -im), (1, 1, re)):
        high, low = split(value)
        rows, cols = pl.ds(row + r * k, k), pl.ds(col + c * n, n)
        high_ref[rows, cols] = high
        low_ref[rows, cols] = low


def panel_factors(held, new, old, inverses, targets, chain, my_row, group):
    block = held.shape[-1]
    row_tiles = held.shape[0] // CBLK
    rows = row_tiles * block

    def kernel(tgt, chain_ref, row_ref, held_in, new_a, new_b, old_a, old_b, inv_ref, high_ref, low_ref, top_ref, *rest):
        held_ref, new_ref, i0h, i0l, i1h, i1l, uh, ul, sem = rest
        odd = lax.rem(row_ref[0], 2)
        copy = pltpu.make_async_copy(held_in, held_ref.at[: CBLK * row_tiles], sem)
        copy.start()
        new_ref[odd] = new_a[...]
        new_ref[1 - odd] = new_b[...]
        fix_chained(chain_ref, new_ref, odd, (old_a, old_b), block)
        store_complex(i0h, i0l, 0, 0, inv_ref[0, 0], inv_ref[0, 1])
        store_complex(i1h, i1l, 0, 0, inv_ref[1, 0], inv_ref[1, 1])
        store_complex(uh, ul, 0, 0, new_ref[0, 2], new_ref[0, 3])
        lower = dot3(
            *split(jnp.concatenate([new_ref[1, 0], new_ref[1, 1]], axis=1)), i0h[...], i0l[...]
        )
        top_ref[...] = lower
        copy.wait()
        replace_rows(tgt, odd, (old_a, old_b), held_ref, block)

        @pl.when(row_ref[0] == 1)
        def _():
            for m in range(CBLK):
                for c in range(2):
                    held_ref[m, c] = new_ref[1, 2 * m + c]

        def one(g, carry):
            x = [
                jnp.concatenate(
                    [
                        jnp.concatenate(
                            [held_ref[(g * group + t) * CBLK + m, 0], held_ref[(g * group + t) * CBLK + m, 1]], axis=1
                        )
                        for t in range(group)
                    ],
                    axis=0,
                )
                for m in range(CBLK)
            ]
            at = pl.ds(pl.multiple_of(g * (group * block), group * block), group * block)
            l0h, l0l = split(dot3(*split(x[0]), i0h[...], i0l[...]))
            high_ref[at, : 2 * block] = l0h
            low_ref[at, : 2 * block] = l0l
            y = x[1] - dot3(l0h, l0l, uh[...], ul[...])
            l1h, l1l = split(dot3(*split(y), i1h[...], i1l[...]))
            high_ref[at, 2 * block :] = l1h
            low_ref[at, 2 * block :] = l1l
            return carry

        lax.fori_loop(0, row_tiles // group, one, 0)

    wide = pltpu.VMEM((2 * block, 2 * block), BF16)
    return call(
        kernel,
        20,
        out_shape=(
            jax.ShapeDtypeStruct((rows, 4 * block), BF16),
            jax.ShapeDtypeStruct((rows, 4 * block), BF16),
            jax.ShapeDtypeStruct((block, 2 * block), F32),
        ),
        in_specs=[SMEM, SMEM, SMEM, HBM] + [VMEM] * 5,
        out_specs=(VMEM, VMEM, VMEM),
        scratch_shapes=[pltpu.VMEM((held.shape[0] + CBLK,) + held.shape[1:], F32), pltpu.VMEM((2, 2 * CBLK, block, block), F32)]
        + [wide] * 6
        + [pltpu.SemaphoreType.DMA],
        name="panel_factors",
    )(targets, chain, my_row, pltpu.with_memory_space_constraint(held, pltpu.HBM), *new, *old, inverses)


def update(held, new, old, high, low, lower_top, targets, chain, my_row, my_col, rows_n, group):
    block = held.shape[-1]
    row_tiles = held.shape[0] // CBLK
    rows = row_tiles * block
    steps = row_tiles // group
    span = group * block

    def kernel(tgt, chain_ref, row_ref, col_ref, held_in, new_a, new_b, old_a, old_b, high_in, low_in, top_ref, out_ref, *rest):
        held_ref, new_ref, high_ref, low_ref, res_ref, wh, wl, sem, in_sems, out_sems = rest
        odd = lax.rem(row_ref[0], 2)
        copy = pltpu.make_async_copy(held_in, held_ref.at[: CBLK * row_tiles], sem)
        copy.start()
        for g in range(steps):
            at = pl.ds(g * span, span)
            for n, (src, dst) in enumerate(((high_in, high_ref), (low_in, low_ref))):
                pltpu.make_async_copy(src.at[at], dst.at[at], in_sems.at[2 * g + n]).start()
        new_ref[odd] = new_a[...]
        new_ref[1 - odd] = new_b[...]
        fix_chained(chain_ref, new_ref, odd, (old_a, old_b), block)
        for m in range(CBLK):
            store_complex(wh, wl, 0, 2 * m * block, new_ref[0, 2 * m], new_ref[0, 2 * m + 1])
        first = dot3(*split(top_ref[...]), wh[: 2 * block, :], wl[: 2 * block, :])
        second = []
        for n in range(2 * CBLK):
            second.append(new_ref[1, n] - first[:, n * block : (n + 1) * block])
            new_ref[1, n] = second[n]
        for m in range(CBLK):
            store_complex(wh, wl, 2 * block, 2 * m * block, second[2 * m], second[2 * m + 1])
        copy.wait()
        replace_rows(tgt, odd, (old_a, old_b), held_ref, block)
        for g in range(steps):
            at = pl.ds(g * span, span)
            for n, (src, dst) in enumerate(((high_in, high_ref), (low_in, low_ref))):
                pltpu.make_async_copy(src.at[at], dst.at[at], in_sems.at[2 * g + n]).wait()
            y = dot3(high_ref[at, :], low_ref[at, :], wh[...], wl[...])
            for t in range(group):
                tile = g * group + t
                for m in range(CBLK):
                    for c in range(2):
                        n = 2 * m + c
                        res_ref[c, tile * block : (tile + 1) * block, m * block : (m + 1) * block] = (
                            held_ref[tile * CBLK + m, c]
                            - y[t * block : (t + 1) * block, n * block : (n + 1) * block]
                        )
            for panel in range(2):

                @pl.when(col_ref[0] == panel)
                def _(panel=panel, at=at):
                    for c in range(2):
                        cols = slice((2 * panel + c) * block, (2 * panel + c + 1) * block)
                        res_ref[c, at, :block] = high_ref[at, cols].astype(F32) + low_ref[at, cols].astype(F32)

            if g == 0:
                for p in range(2):

                    @pl.when(row_ref[0] == p)
                    def _(p=p):
                        for c in range(2):
                            for m in range(CBLK):
                                res_ref[c, :block, m * block : (m + 1) * block] = new_ref[p, 2 * m + c]

                @pl.when((row_ref[0] == 1) & (col_ref[0] == 0))
                def _():
                    for c in range(2):
                        res_ref[c, :block, :block] = top_ref[:, c * block : (c + 1) * block]

            for c in range(2):
                pltpu.make_async_copy(res_ref.at[c, at], out_ref.at[c, at], out_sems.at[2 * g + c]).start()
        for g in range(steps):
            at = pl.ds(g * span, span)
            for c in range(2):
                pltpu.make_async_copy(res_ref.at[c, at], out_ref.at[c, at], out_sems.at[2 * g + c]).wait()

    return call(
        kernel,
        24,
        out_shape=jax.ShapeDtypeStruct((2, rows, CBLK * block), F32),
        in_specs=[SMEM] * 4 + [HBM] + [VMEM] * 4 + [ANY] * 2 + [VMEM],
        out_specs=ANY,
        scratch_shapes=[
            pltpu.VMEM((held.shape[0] + CBLK,) + held.shape[1:], F32),
            pltpu.VMEM((2, 2 * CBLK, block, block), F32),
            pltpu.VMEM((rows, 4 * block), BF16),
            pltpu.VMEM((rows, 4 * block), BF16),
            pltpu.VMEM((2, rows, CBLK * block), F32),
            pltpu.VMEM((4 * block, 4 * block), BF16),
            pltpu.VMEM((4 * block, 4 * block), BF16),
            pltpu.SemaphoreType.DMA,
            pltpu.SemaphoreType.DMA((2 * steps,)),
            pltpu.SemaphoreType.DMA((2 * steps,)),
        ],
        name="update",
    )(
        targets, chain, my_row, my_col, pltpu.with_memory_space_constraint(held, pltpu.HBM), *new, *old, high, low, lower_top
    )


def per_device(assembly, slot_tile, pivots, inverses):
    cols_n = lax.axis_size("pcol")
    rows_n = lax.axis_size("prow")
    my_col = lax.axis_index("pcol")
    my_row = lax.axis_index("prow")
    tiles = assembly[0]
    slots = tiles.shape[0]
    block = tiles.shape[-1]
    row_tiles = slots // CBLK
    base = (slots + cols_n - 1) // cols_n
    excess_max = slots // (base + 1)
    depth = cols_n // LINES
    group = 4 if row_tiles % 4 == 0 else 1
    level = my_col // LINES
    me = my_col.astype(jnp.int32).reshape(1)
    me_row = my_row.astype(jnp.int32).reshape(1)
    odd = me_row % 2
    ids = slot_tile[0]

    picks = jnp.arange(2 * block, dtype=jnp.int32)
    first, second = pivots[0], pivots[1]
    same = (second[:, None] == first[None, :]) & (first[None, :] >= 2 * block)
    chained = jnp.sum(jnp.where(same, picks[None, :block], 0), axis=1)
    second_source = jnp.where(jnp.any(same, axis=1), chained, second)
    replaced = jnp.any(same, axis=0)
    wanted = jnp.concatenate([first, second_source])
    named = jnp.concatenate([first, second])
    moved = (named != picks) & ~jnp.concatenate([replaced, jnp.zeros_like(replaced)])

    def local_row(row, keep):
        ours = (row // block % rows_n == my_row) & keep
        return jnp.where(ours, row // block // rows_n * block + row % block, -1)

    source_rows = local_row(wanted, True)
    targets = local_row(named, moved)
    away = named // block % rows_n >= 2
    far = jnp.where(my_row % 2 == 0, away[:block], away[block:])
    fix = jnp.any(same, axis=1) & away[block:] & (my_row >= 2) & (rows_n == 4)
    chain = jnp.concatenate([jnp.where(fix, chained, -1), jnp.sum(fix.astype(jnp.int32))[None]])

    def after(values, earlier):
        return lax.optimization_barrier((tuple(values), tuple(earlier)))[0]

    def swapped(phase):
        due = []
        for z in range(depth):
            chunks = []
            for t in range(1, depth):
                chunks += [("up", t)] * (z - t >= 0) + [("down", t)] * (z + t < depth)
            due.append(chunks[phase - 2])
        return due

    def shift_pairs(k, phase):
        zm, dx = k // LINES, k % LINES
        pairs = []
        for i in range(cols_n):
            if dx == 0 and zm >= 2 and (i ^ k) // LINES < depth - 1:
                due = depth - 1
            elif zm == depth - 1 or (dx == 0 and zm == 1):
                due = depth
            else:
                due = depth + 1
            if (i ^ k) >= LINES and due == phase:
                pairs.append((i, i ^ k))
        return pairs

    packed, shifted, meta = pack(tiles, ids, me, cols_n, base, excess_max)
    parts, origins = [packed], [(0, False)]
    chunk = {("up", 0): packed, ("down", 0): packed}
    arrived, arrived_from = [], []
    done, work = [], []
    near = meta[None]
    for phase in range(1, depth + 2):
        last, work = work, []
        if phase < depth:
            t = phase
            up = [(i, i + LINES) for i in range((t - 1) * LINES, cols_n - LINES)]
            down = [(i, i - LINES) for i in range(LINES, cols_n - (t - 1) * LINES)]
            work.append((chunk["up", t - 1], up, ("up", t), (-t, False)))
            work.append((chunk["down", t - 1], down, ("down", t), (t, False)))
        if phase == 1:
            work.append((packed, [(i, i ^ 1) for i in range(cols_n)], None, (0, True)))
        elif phase <= depth:
            due = swapped(phase)
            keys = sorted(set(due))
            if len(keys) <= 2:
                for key in keys:
                    levels = [z for z in range(depth) if due[z] == key]
                    pairs = [(i, i ^ 1) for z in levels for i in range(z * LINES, (z + 1) * LINES)]
                    steps = tuple(
                        (-key[1] if key[0] == "up" else key[1]) if z in levels else depth for z in range(depth)
                    )
                    work.append((chunk[key], pairs, None, (steps, True)))
            else:
                x = chunk[due[0]]
                for key in keys:
                    if key != due[0]:
                        levels = [level == z for z in range(depth) if due[z] == key]
                        x = jnp.where(functools.reduce(jnp.logical_or, levels), chunk[key], x)
                steps = tuple(-t if d == "up" else t for d, t in due)
                work.append((x, [(i, i ^ 1) for i in range(cols_n)], None, (steps, True)))
        else:
            gathered_all = [got for got, w in zip(done, last) if not isinstance(w[2], int)]
            shifted_first = [got for got, w in zip(done, last) if isinstance(w[2], int)]
        for k in range(1, cols_n):
            pairs = shift_pairs(k, phase)
            if pairs:
                work.append((shifted[k - 1], pairs, k, pairs))
        before = done
        values = after([w[0] for w in work], done) if done else [w[0] for w in work]
        done = [lax.ppermute(x, "pcol", w[1]) for x, w in zip(values, work)]
        for got, (_, _, key, origin) in zip(done, work):
            if isinstance(key, int):
                arrived.append(got)
                arrived_from.append((key, origin))
            else:
                parts.append(got)
                origins.append(origin)
                if key is not None:
                    chunk[key] = got
        step = 1 << (phase - 1)
        if step < cols_n:
            if phase > 1:
                near = after([near], before)[0]
            got = lax.ppermute(near, "pcol", [(i, i ^ step) for i in range(cols_n)])
            near = jnp.concatenate([near, got])
            done = done + [got]
        if phase == 1:
            done = done + [source_rows, targets, far, chain]
    most = jnp.max(near[:, cols_n * base + excess_max])

    def gather_rest():
        mine = meta[cols_n * base + 1 : cols_n * base + excess_max]
        slot = jnp.sum(
            jnp.where(mine[:, None] == ids[None, :], jnp.arange(slots, dtype=jnp.int32)[None, :], 0), axis=1
        )
        rest = jnp.stack(
            [lax.dynamic_index_in_dim(tiles, slot[e], 0, False) for e in range(excess_max - 1)]
        )
        others = [
            lax.ppermute(rest, "pcol", [(i, i ^ k) for i in range(cols_n)]) for k in range(1, cols_n)
        ]
        return jnp.concatenate([rest] + others)

    def no_rest():
        return unwritten((cols_n * (excess_max - 1),) + tiles.shape[1:])

    rest = lax.cond(most > 1, gather_rest, no_rest)

    late_rows = after([source_rows], gathered_all)[0]
    held_p, keep_p, send_p, top_p = extract(
        parts, origins, rest, near, ids, late_rows, me, odd, cols_n, base
    )
    new_p, old_p, crossed = exchange(keep_p, send_p, top_p, far, my_row, rows_n, shifted_first)
    high, low, lower_top = panel_factors(held_p, new_p, old_p, inverses, targets, chain, me_row, group)

    late_rows = after([source_rows], [crossed])[0]
    held, keep, send, top = extract(
        parts, origins, rest, near, ids, late_rows, me, odd, cols_n, base, tiles, arrived, arrived_from
    )
    new, old, _ = exchange(keep, send, top, far, my_row, rows_n, meanwhile=high)
    return update(held, new, old, high, low, lower_top, targets, chain, me_row, me, rows_n, group)


def solution(mesh):
    in_specs = (P("prow", "pcol", None, None, None), P("prow", "pcol"), P(), P())
    out_specs = P(None, "prow", "pcol")
    return jax.shard_map(
        per_device, mesh=mesh, in_specs=in_specs, out_specs=out_specs, check_vma=False
    )
```

```python
import functools

import jax
import jax.numpy as jnp
from jax import lax
from jax.experimental import pallas as pl
from jax.experimental.pallas import tpu as pltpu
from jax.sharding import PartitionSpec as P

CBLK = 2
LINES = 2
F32 = jnp.float32
BF16 = jnp.bfloat16
MIB = 1024 * 1024
META = 128

ANY = pl.BlockSpec(memory_space=pl.ANY)
SMEM = pl.BlockSpec(memory_space=pltpu.SMEM)
VMEM = pl.BlockSpec(memory_space=pltpu.VMEM)
HBM = pl.BlockSpec(memory_space=pltpu.HBM)


def call(kernel, mib, **kw):
    return pl.pallas_call(
        kernel,
        compiler_params=pltpu.CompilerParams(vmem_limit_bytes=mib * MIB),
        cost_estimate=pl.CostEstimate(flops=0, bytes_accessed=0, transcendentals=0),
        **kw,
    )


def list_slots(ids_ref, pos, meta, slots, cols_n, base, excess_max):
    first = cols_n * base
    for n in range(first + excess_max):
        meta[n] = -1
        pos[n] = 0
    for o in range(cols_n + 1):
        pos[first + excess_max + o] = 0

    def one(j, carry):
        t = ids_ref[j]
        owner = t & (cols_n - 1)
        r = pos[first + excess_max + owner]
        pos[first + excess_max + owner] = r + 1
        e = pos[first + excess_max + cols_n]
        over = (r >= base).astype(jnp.int32)
        pos[first + excess_max + cols_n] = e + over
        at = jnp.where(r >= base, first + e, owner * base + r)
        pos[at] = j
        meta[at] = t
        return carry

    lax.fori_loop(0, slots, one, 0)
    meta[first + excess_max] = pos[first + excess_max + cols_n]


def pack(tiles, ids, me, cols_n, base, excess_max):
    slots = tiles.shape[0]
    count = LINES * base + 1
    first = cols_n * base

    def kernel(ids_ref, me_ref, tiles_ref, stream_ref, *rest):
        outs, (meta, held, pos, sems) = rest[: cols_n - 1], rest[cols_n - 1 :]
        list_slots(ids_ref, pos, meta, slots, cols_n, base, excess_max)
        moves = []
        for n in range(count):
            at = n if n < LINES * base else first
            moves.append((meta[at] >= 0, pos[at], stream_ref.at[n]))
        for k in range(1, cols_n):
            owner = me_ref[0] ^ k
            for r in range(base):
                at = owner * base + r
                moves.append(((meta[at] >= 0) & (owner >= LINES), pos[at], outs[k - 1].at[r]))
        for n, (cond, slot, _) in enumerate(moves):

            @pl.when(cond)
            def _(n=n, slot=slot):
                pltpu.make_async_copy(tiles_ref.at[slot], held.at[n], sems.at[0, n]).start()

        for n, (cond, slot, dst) in enumerate(moves):

            @pl.when(cond)
            def _(n=n, slot=slot, dst=dst):
                pltpu.make_async_copy(tiles_ref.at[slot], held.at[n], sems.at[0, n]).wait()
                pltpu.make_async_copy(held.at[n], dst, sems.at[1, n]).start()

        for n, (cond, _, dst) in enumerate(moves):

            @pl.when(cond)
            def _(n=n, dst=dst):
                pltpu.make_async_copy(held.at[n], dst, sems.at[1, n]).wait()

    one = tiles.shape[1:]
    total = count + (cols_n - 1) * base
    got = call(
        kernel,
        8,
        out_shape=(pltpu.HBM((count,) + one, F32),)
        + tuple(pltpu.HBM((base,) + one, F32) for _ in range(1, cols_n))
        + (jax.ShapeDtypeStruct((META,), jnp.int32),),
        in_specs=[SMEM, SMEM, HBM],
        out_specs=tuple(HBM for _ in range(cols_n)) + (SMEM,),
        scratch_shapes=[
            pltpu.VMEM((total,) + one, F32),
            pltpu.SMEM((first + excess_max + cols_n + 1,), jnp.int32),
            pltpu.SemaphoreType.DMA((2, total)),
        ],
        name="pack",
    )(ids, me, tiles)
    return got[0], got[1:-1], got[-1]


def unwritten(shape):
    def kernel(out_ref):
        pass

    return call(kernel, 2, out_shape=jax.ShapeDtypeStruct(shape, F32), out_specs=HBM, name="unwritten")()


def extract(
    parts, origins, rest, near, ids, source_rows, me, odd, cols_n, base, tiles=None, arrived=(), arrived_from=()
):
    block = rest.shape[-1]
    bits = block.bit_length() - 1
    width = CBLK * cols_n
    width_bits, cols_bits = width.bit_length() - 1, cols_n.bit_length() - 1
    wide = 2 * CBLK
    own = tiles is not None
    count = LINES * base + 1
    depth = cols_n // LINES
    tiles_n = ids.shape[0]
    first = cols_n * base
    per = rest.shape[0] // cols_n

    def kernel(near_ref, ids_ref, rows_ref, me_ref, odd_ref, *rest_refs):
        part_refs, rest_refs = rest_refs[: len(parts)], rest_refs[len(parts) :]
        rest_ref, rest_refs = rest_refs[0], rest_refs[1:]
        if own:
            tiles_ref, arrived_refs = rest_refs[0], rest_refs[1 : 1 + len(arrived)]
        held_out, keep, send, top, held, sem, out_sem = rest_refs[-7:]
        me = me_ref[0]
        level, line = lax.shift_right_logical(me, 1), me & 1
        gathered = me < LINES

        def fetch(src, t, wanted):
            column = t & (width - 1)
            row = lax.shift_right_logical(t, width_bits)
            if own:
                ours = (column & (cols_n - 1)) == me
                place = row * CBLK + lax.shift_right_logical(column, cols_bits)
            else:
                ours = column < LINES
                place = row * CBLK + column

            @pl.when((t >= 0) & ours & wanted)
            def _():
                pltpu.make_async_copy(src, held.at[place], sem).start()

        if own:

            @pl.when(~gathered)
            def _():
                def one(j, carry):
                    fetch(tiles_ref.at[j], ids_ref[j], True)
                    return carry

                lax.fori_loop(0, tiles_n, one, 0)
                for ref, (k, pairs) in zip(arrived_refs, arrived_from):
                    here = functools.reduce(jnp.logical_or, [me == b for _, b in pairs])
                    for r in range(base):
                        fetch(ref.at[r], near_ref[k, me * base + r], here)

        for ref, (step, cross) in zip(part_refs, origins):
            if isinstance(step, tuple):
                by_level = step[0]
                for z in range(1, depth):
                    by_level = jnp.where(level == z, step[z], by_level)
                step = by_level
            at = level + step
            valid = (at >= 0) & (at < depth)
            source = at * LINES + (1 - line if cross else line)
            if own:
                valid = valid & (gathered | (source != me))

            @pl.when(valid)
            def _(ref=ref, source=source):
                k = source ^ me

                def streams():
                    for q in range(count - 1):
                        fetch(ref.at[q], near_ref[k, q], True)

                if own:
                    pl.when(gathered)(streams)
                else:
                    streams()
                fetch(ref.at[count - 1], near_ref[k, first], True)

        most = near_ref[0, first + per + 1]
        for k in range(1, cols_n):
            most = jnp.maximum(most, near_ref[k, first + per + 1])

        @pl.when(most > 1)
        def _():
            for k in range(cols_n):

                def one(e, carry, k=k):
                    fetch(rest_ref.at[k * per + e], near_ref[k, first + 1 + e], (gathered | (k > 0)) if own else True)
                    return carry

                lax.fori_loop(0, per, one, 0)

        pltpu.make_async_copy(held, held, sem).wait()
        copy_out = pltpu.make_async_copy(held, held_out, out_sem)
        copy_out.start()
        for m in range(CBLK):
            for c in range(2):
                top[2 * m + c] = held[m, c]
        for out, half in ((keep, odd_ref[0]), (send, 1 - odd_ref[0])):

            def pick(j, carry, out=out, half=half):
                row = rows_ref[half * block + j]
                here = row >= 0
                row = jnp.maximum(row, 0)
                tile = lax.shift_right_logical(row, bits) * CBLK
                inner = row & (block - 1)
                for m in range(CBLK):
                    for c in range(2):
                        value = held[tile + m, c, pl.ds(inner, 1), :]
                        out[2 * m + c, pl.ds(j, 1), :] = jnp.where(here, value, 0.0)
                return carry

            lax.fori_loop(0, block, pick, 0, unroll=8)
        copy_out.wait()

    part_rows = jax.ShapeDtypeStruct((wide, block, block), F32)
    operands = list(parts) + [rest] + ([tiles] + list(arrived) if own else [])
    operands = [pltpu.with_memory_space_constraint(x, pltpu.HBM) for x in operands]
    return call(
        kernel,
        12,
        out_shape=(pltpu.HBM((tiles_n, 2, block, block), F32), part_rows, part_rows, part_rows),
        in_specs=[SMEM] * 5 + [HBM] * len(operands),
        out_specs=(HBM, VMEM, VMEM, VMEM),
        scratch_shapes=[
            pltpu.VMEM((tiles_n, 2, block, block), F32),
            pltpu.SemaphoreType.DMA,
            pltpu.SemaphoreType.DMA,
        ],
        name="own_rows" if own else "panel_rows",
    )(near, ids, source_rows, me, odd, *operands)


def exchange(keep, send, top, far, my_row, rows_n, earlier=(), meanwhile=None):
    def cross(x, step):
        return lax.ppermute(x, "prow", [(p, p ^ step) for p in range(rows_n)])

    total = keep + cross(send, 1)
    if rows_n == 4:
        there = far[None, :, None]
        second = my_row >= 2
        message = jnp.where(there & ~second, top, total)
        message = lax.optimization_barrier((message, tuple(earlier)))[0]
        got = cross(message, 2)
        if meanwhile is not None:
            got = lax.optimization_barrier((got, meanwhile))[0]
        total = total + jnp.where(there & second, 0.0, got)
        held = jnp.where(second, got, top)
        return (total, cross(total, 1)), (held, cross(held, 1)), got
    held = top
    step = 2
    while step < rows_n:
        got = lax.ppermute(held, "prow", [(p, p + step) for p in range(step)])
        held = jnp.where((my_row >= step) & (my_row < 2 * step), got, held)
        total = total + cross(total, step)
        step *= 2
    return (total, cross(total, 1)), (held, cross(held, 1)), total


def fix_chained(chain_ref, new_ref, odd, old_refs, block):
    @pl.when(chain_ref[block] > 0)
    def _():
        def one(i, carry):
            j = chain_ref[i]

            @pl.when((j >= 0) & (odd == 0))
            def _():
                new_ref[1, :, pl.ds(i, 1), :] = old_refs[0][:, pl.ds(j, 1), :]

            @pl.when((j >= 0) & (odd == 1))
            def _():
                new_ref[1, :, pl.ds(i, 1), :] = old_refs[1][:, pl.ds(j, 1), :]

            return carry

        lax.fori_loop(0, block, one, 0)


def replace_rows(targets_ref, odd, old_refs, held, block):
    bits = block.bit_length() - 1

    spare = held.shape[0] - CBLK
    for ref, half in ((old_refs[0], odd), (old_refs[1], 1 - odd)):

        def one(j, carry, ref=ref, half=half):
            row = targets_ref[half * block + j]
            tile = jnp.where(row >= 0, lax.shift_right_logical(row, bits) * CBLK, spare)
            inner = row & (block - 1)
            for m in range(CBLK):
                for c in range(2):
                    held[tile + m, c, pl.ds(inner, 1), :] = ref[2 * m + c, pl.ds(j, 1), :]
            return carry

        lax.fori_loop(0, block, one, 0, unroll=8)


def split(x):
    high = x.astype(BF16)
    return high, (x - high.astype(F32)).astype(BF16)


def dot3(high, low, w_high, w_low):
    return (
        jnp.dot(high, w_high, preferred_element_type=F32)
        + jnp.dot(high, w_low, preferred_element_type=F32)
        + jnp.dot(low, w_high, preferred_element_type=F32)
    )


def store_complex(high_ref, low_ref, row, col, re, im):
    k, n = re.shape
    for r, c, value in ((0, 0, re), (0, 1, im), (1, 0, -im), (1, 1, re)):
        high, low = split(value)
        rows, cols = pl.ds(row + r * k, k), pl.ds(col + c * n, n)
        high_ref[rows, cols] = high
        low_ref[rows, cols] = low


def panel_factors(held, new, old, inverses, targets, chain, my_row, group):
    block = held.shape[-1]
    row_tiles = held.shape[0] // CBLK
    rows = row_tiles * block

    def kernel(tgt, chain_ref, row_ref, held_in, new_a, new_b, old_a, old_b, inv_ref, high_ref, low_ref, top_ref, *rest):
        held_ref, new_ref, i0h, i0l, i1h, i1l, uh, ul, sem = rest
        odd = lax.rem(row_ref[0], 2)
        copy = pltpu.make_async_copy(held_in, held_ref.at[: CBLK * row_tiles], sem)
        copy.start()
        new_ref[odd] = new_a[...]
        new_ref[1 - odd] = new_b[...]
        fix_chained(chain_ref, new_ref, odd, (old_a, old_b), block)
        store_complex(i0h, i0l, 0, 0, inv_ref[0, 0], inv_ref[0, 1])
        store_complex(i1h, i1l, 0, 0, inv_ref[1, 0], inv_ref[1, 1])
        store_complex(uh, ul, 0, 0, new_ref[0, 2], new_ref[0, 3])
        lower = dot3(
            *split(jnp.concatenate([new_ref[1, 0], new_ref[1, 1]], axis=1)), i0h[...], i0l[...]
        )
        top_ref[...] = lower
        copy.wait()
        replace_rows(tgt, odd, (old_a, old_b), held_ref, block)

        @pl.when(row_ref[0] == 1)
        def _():
            for m in range(CBLK):
                for c in range(2):
                    held_ref[m, c] = new_ref[1, 2 * m + c]

        def one(g, carry):
            x = [
                jnp.concatenate(
                    [
                        jnp.concatenate(
                            [held_ref[(g * group + t) * CBLK + m, 0], held_ref[(g * group + t) * CBLK + m, 1]], axis=1
                        )
                        for t in range(group)
                    ],
                    axis=0,
                )
                for m in range(CBLK)
            ]
            at = pl.ds(pl.multiple_of(g * (group * block), group * block), group * block)
            l0h, l0l = split(dot3(*split(x[0]), i0h[...], i0l[...]))
            high_ref[at, : 2 * block] = l0h
            low_ref[at, : 2 * block] = l0l
            y = x[1] - dot3(l0h, l0l, uh[...], ul[...])
            l1h, l1l = split(dot3(*split(y), i1h[...], i1l[...]))
            high_ref[at, 2 * block :] = l1h
            low_ref[at, 2 * block :] = l1l
            return carry

        lax.fori_loop(0, row_tiles // group, one, 0)

    wide = pltpu.VMEM((2 * block, 2 * block), BF16)
    return call(
        kernel,
        20,
        out_shape=(
            jax.ShapeDtypeStruct((rows, 4 * block), BF16),
            jax.ShapeDtypeStruct((rows, 4 * block), BF16),
            jax.ShapeDtypeStruct((block, 2 * block), F32),
        ),
        in_specs=[SMEM, SMEM, SMEM, HBM] + [VMEM] * 5,
        out_specs=(VMEM, VMEM, VMEM),
        scratch_shapes=[pltpu.VMEM((held.shape[0] + CBLK,) + held.shape[1:], F32), pltpu.VMEM((2, 2 * CBLK, block, block), F32)]
        + [wide] * 6
        + [pltpu.SemaphoreType.DMA],
        name="panel_factors",
    )(targets, chain, my_row, pltpu.with_memory_space_constraint(held, pltpu.HBM), *new, *old, inverses)


def update(held, new, old, high, low, lower_top, targets, chain, my_row, my_col, rows_n, group):
    block = held.shape[-1]
    row_tiles = held.shape[0] // CBLK
    rows = row_tiles * block
    steps = row_tiles // group
    span = group * block

    def kernel(tgt, chain_ref, row_ref, col_ref, held_in, new_a, new_b, old_a, old_b, high_in, low_in, top_ref, out_ref, *rest):
        held_ref, new_ref, high_ref, low_ref, res_ref, wh, wl, sem, in_sems, out_sems = rest
        odd = lax.rem(row_ref[0], 2)
        copy = pltpu.make_async_copy(held_in, held_ref.at[: CBLK * row_tiles], sem)
        copy.start()
        for g in range(steps):
            at = pl.ds(g * span, span)
            for n, (src, dst) in enumerate(((high_in, high_ref), (low_in, low_ref))):
                pltpu.make_async_copy(src.at[at], dst.at[at], in_sems.at[2 * g + n]).start()
        new_ref[odd] = new_a[...]
        new_ref[1 - odd] = new_b[...]
        fix_chained(chain_ref, new_ref, odd, (old_a, old_b), block)
        for m in range(CBLK):
            store_complex(wh, wl, 0, 2 * m * block, new_ref[0, 2 * m], new_ref[0, 2 * m + 1])
        first = dot3(*split(top_ref[...]), wh[: 2 * block, :], wl[: 2 * block, :])
        second = []
        for n in range(2 * CBLK):
            second.append(new_ref[1, n] - first[:, n * block : (n + 1) * block])
            new_ref[1, n] = second[n]
        for m in range(CBLK):
            store_complex(wh, wl, 2 * block, 2 * m * block, second[2 * m], second[2 * m + 1])
        copy.wait()
        replace_rows(tgt, odd, (old_a, old_b), held_ref, block)
        for g in range(steps):
            at = pl.ds(g * span, span)
            for n, (src, dst) in enumerate(((high_in, high_ref), (low_in, low_ref))):
                pltpu.make_async_copy(src.at[at], dst.at[at], in_sems.at[2 * g + n]).wait()
            y = dot3(high_ref[at, :], low_ref[at, :], wh[...], wl[...])
            for t in range(group):
                tile = g * group + t
                for m in range(CBLK):
                    for c in range(2):
                        n = 2 * m + c
                        res_ref[c, tile * block : (tile + 1) * block, m * block : (m + 1) * block] = (
                            held_ref[tile * CBLK + m, c]
                            - y[t * block : (t + 1) * block, n * block : (n + 1) * block]
                        )
            for panel in range(2):

                @pl.when(col_ref[0] == panel)
                def _(panel=panel, at=at):
                    for c in range(2):
                        cols = slice((2 * panel + c) * block, (2 * panel + c + 1) * block)
                        res_ref[c, at, :block] = high_ref[at, cols].astype(F32) + low_ref[at, cols].astype(F32)

            if g == 0:
                for p in range(2):

                    @pl.when(row_ref[0] == p)
                    def _(p=p):
                        for c in range(2):
                            for m in range(CBLK):
                                res_ref[c, :block, m * block : (m + 1) * block] = new_ref[p, 2 * m + c]

                @pl.when((row_ref[0] == 1) & (col_ref[0] == 0))
                def _():
                    for c in range(2):
                        res_ref[c, :block, :block] = top_ref[:, c * block : (c + 1) * block]

            for c in range(2):
                pltpu.make_async_copy(res_ref.at[c, at], out_ref.at[c, at], out_sems.at[2 * g + c]).start()
        for g in range(steps):
            at = pl.ds(g * span, span)
            for c in range(2):
                pltpu.make_async_copy(res_ref.at[c, at], out_ref.at[c, at], out_sems.at[2 * g + c]).wait()

    return call(
        kernel,
        24,
        out_shape=jax.ShapeDtypeStruct((2, rows, CBLK * block), F32),
        in_specs=[SMEM] * 4 + [HBM] + [VMEM] * 4 + [ANY] * 2 + [VMEM],
        out_specs=ANY,
        scratch_shapes=[
            pltpu.VMEM((held.shape[0] + CBLK,) + held.shape[1:], F32),
            pltpu.VMEM((2, 2 * CBLK, block, block), F32),
            pltpu.VMEM((rows, 4 * block), BF16),
            pltpu.VMEM((rows, 4 * block), BF16),
            pltpu.VMEM((2, rows, CBLK * block), F32),
            pltpu.VMEM((4 * block, 4 * block), BF16),
            pltpu.VMEM((4 * block, 4 * block), BF16),
            pltpu.SemaphoreType.DMA,
            pltpu.SemaphoreType.DMA((2 * steps,)),
            pltpu.SemaphoreType.DMA((2 * steps,)),
        ],
        name="update",
    )(
        targets, chain, my_row, my_col, pltpu.with_memory_space_constraint(held, pltpu.HBM), *new, *old, high, low, lower_top
    )


def per_device(assembly, slot_tile, pivots, inverses):
    cols_n = lax.axis_size("pcol")
    rows_n = lax.axis_size("prow")
    my_col = lax.axis_index("pcol")
    my_row = lax.axis_index("prow")
    tiles = assembly[0]
    slots = tiles.shape[0]
    block = tiles.shape[-1]
    row_tiles = slots // CBLK
    base = (slots + cols_n - 1) // cols_n
    excess_max = slots // (base + 1)
    depth = cols_n // LINES
    group = 4 if row_tiles % 4 == 0 else 1
    level = my_col // LINES
    me = my_col.astype(jnp.int32).reshape(1)
    me_row = my_row.astype(jnp.int32).reshape(1)
    odd = me_row % 2
    ids = slot_tile[0]

    picks = jnp.arange(2 * block, dtype=jnp.int32)
    first, second = pivots[0], pivots[1]
    same = (second[:, None] == first[None, :]) & (first[None, :] >= 2 * block)
    chained = jnp.sum(jnp.where(same, picks[None, :block], 0), axis=1)
    second_source = jnp.where(jnp.any(same, axis=1), chained, second)
    replaced = jnp.any(same, axis=0)
    wanted = jnp.concatenate([first, second_source])
    named = jnp.concatenate([first, second])
    moved = (named != picks) & ~jnp.concatenate([replaced, jnp.zeros_like(replaced)])

    def local_row(row, keep):
        ours = (row // block % rows_n == my_row) & keep
        return jnp.where(ours, row // block // rows_n * block + row % block, -1)

    source_rows = local_row(wanted, True)
    targets = local_row(named, moved)
    away = named // block % rows_n >= 2
    far = jnp.where(my_row % 2 == 0, away[:block], away[block:])
    fix = jnp.any(same, axis=1) & away[block:] & (my_row >= 2) & (rows_n == 4)
    chain = jnp.concatenate([jnp.where(fix, chained, -1), jnp.sum(fix.astype(jnp.int32))[None]])

    def after(values, earlier):
        return lax.optimization_barrier((tuple(values), tuple(earlier)))[0]

    def swapped(phase):
        due = []
        for z in range(depth):
            chunks = []
            for t in range(1, depth):
                chunks += [("up", t)] * (z - t >= 0) + [("down", t)] * (z + t < depth)
            due.append(chunks[phase - 2])
        return due

    def shift_pairs(k, phase):
        zm, dx = k // LINES, k % LINES
        pairs = []
        for i in range(cols_n):
            if dx == 0 and zm >= 2 and (i ^ k) // LINES < depth - 1:
                due = depth - 1
            elif zm == depth - 1 or (dx == 0 and zm == 1):
                due = depth
            else:
                due = depth + 1
            if (i ^ k) >= LINES and due == phase:
                pairs.append((i, i ^ k))
        return pairs

    packed, shifted, meta = pack(tiles, ids, me, cols_n, base, excess_max)
    parts, origins = [packed], [(0, False)]
    chunk = {("up", 0): packed, ("down", 0): packed}
    arrived, arrived_from = [], []
    done, work = [], []
    near = meta[None]
    for phase in range(1, depth + 2):
        last, work = work, []
        if phase < depth:
            t = phase
            up = [(i, i + LINES) for i in range((t - 1) * LINES, cols_n - LINES)]
            down = [(i, i - LINES) for i in range(LINES, cols_n - (t - 1) * LINES)]
            work.append((chunk["up", t - 1], up, ("up", t), (-t, False)))
            work.append((chunk["down", t - 1], down, ("down", t), (t, False)))
        if phase == 1:
            work.append((packed, [(i, i ^ 1) for i in range(cols_n)], None, (0, True)))
        elif phase <= depth:
            due = swapped(phase)
            keys = sorted(set(due))
            if len(keys) <= 2:
                for key in keys:
                    levels = [z for z in range(depth) if due[z] == key]
                    pairs = [(i, i ^ 1) for z in levels for i in range(z * LINES, (z + 1) * LINES)]
                    steps = tuple(
                        (-key[1] if key[0] == "up" else key[1]) if z in levels else depth for z in range(depth)
                    )
                    work.append((chunk[key], pairs, None, (steps, True)))
            else:
                x = chunk[due[0]]
                for key in keys:
                    if key != due[0]:
                        levels = [level == z for z in range(depth) if due[z] == key]
                        x = jnp.where(functools.reduce(jnp.logical_or, levels), chunk[key], x)
                steps = tuple(-t if d == "up" else t for d, t in due)
                work.append((x, [(i, i ^ 1) for i in range(cols_n)], None, (steps, True)))
        else:
            gathered_all = [got for got, w in zip(done, last) if not isinstance(w[2], int)]
            shifted_first = [got for got, w in zip(done, last) if isinstance(w[2], int)]
        for k in reversed(range(1, cols_n)):
            pairs = shift_pairs(k, phase)
            if pairs:
                work.append((shifted[k - 1], pairs, k, pairs))
        before = done
        values = after([w[0] for w in work], done) if done else [w[0] for w in work]
        done = [lax.ppermute(x, "pcol", w[1]) for x, w in zip(values, work)]
        for got, (_, _, key, origin) in zip(done, work):
            if isinstance(key, int):
                arrived.append(got)
                arrived_from.append((key, origin))
            else:
                parts.append(got)
                origins.append(origin)
                if key is not None:
                    chunk[key] = got
        step = 1 << (phase - 1)
        if step < cols_n:
            if phase > 1:
                near = after([near], before)[0]
            got = lax.ppermute(near, "pcol", [(i, i ^ step) for i in range(cols_n)])
            near = jnp.concatenate([near, got])
            done = done + [got]
        if phase == 1:
            done = done + [source_rows, targets, far, chain]
    most = jnp.max(near[:, cols_n * base + excess_max])

    def gather_rest():
        mine = meta[cols_n * base + 1 : cols_n * base + excess_max]
        slot = jnp.sum(
            jnp.where(mine[:, None] == ids[None, :], jnp.arange(slots, dtype=jnp.int32)[None, :], 0), axis=1
        )
        rest = jnp.stack(
            [lax.dynamic_index_in_dim(tiles, slot[e], 0, False) for e in range(excess_max - 1)]
        )
        others = [
            lax.ppermute(rest, "pcol", [(i, i ^ k) for i in range(cols_n)]) for k in range(1, cols_n)
        ]
        return jnp.concatenate([rest] + others)

    def no_rest():
        return unwritten((cols_n * (excess_max - 1),) + tiles.shape[1:])

    rest = lax.cond(most > 1, gather_rest, no_rest)

    late_rows = after([source_rows], gathered_all)[0]
    held_p, keep_p, send_p, top_p = extract(
        parts, origins, rest, near, ids, late_rows, me, odd, cols_n, base
    )
    new_p, old_p, crossed = exchange(keep_p, send_p, top_p, far, my_row, rows_n, shifted_first)
    high, low, lower_top = panel_factors(held_p, new_p, old_p, inverses, targets, chain, me_row, group)

    late_rows = after([source_rows], [crossed])[0]
    held, keep, send, top = extract(
        parts, origins, rest, near, ids, late_rows, me, odd, cols_n, base, tiles, arrived, arrived_from
    )
    new, old, _ = exchange(keep, send, top, far, my_row, rows_n, meanwhile=high)
    return update(held, new, old, high, low, lower_top, targets, chain, me_row, me, rows_n, group)


def solution(mesh):
    in_specs = (P("prow", "pcol", None, None, None), P("prow", "pcol"), P(), P())
    out_specs = P(None, "prow", "pcol")
    return jax.shard_map(
        per_device, mesh=mesh, in_specs=in_specs, out_specs=out_specs, check_vma=False
    )
```

```python
import functools

import jax
import jax.numpy as jnp
from jax import lax
from jax.experimental import pallas as pl
from jax.experimental.pallas import tpu as pltpu
from jax.sharding import PartitionSpec as P

CBLK = 2
LINES = 2
F32 = jnp.float32
BF16 = jnp.bfloat16
MIB = 1024 * 1024
META = 128

ANY = pl.BlockSpec(memory_space=pl.ANY)
SMEM = pl.BlockSpec(memory_space=pltpu.SMEM)
VMEM = pl.BlockSpec(memory_space=pltpu.VMEM)
HBM = pl.BlockSpec(memory_space=pltpu.HBM)


def call(kernel, mib, **kw):
    return pl.pallas_call(
        kernel,
        compiler_params=pltpu.CompilerParams(vmem_limit_bytes=mib * MIB),
        cost_estimate=pl.CostEstimate(flops=0, bytes_accessed=0, transcendentals=0),
        **kw,
    )


def list_slots(ids_ref, pos, meta, slots, cols_n, base, excess_max):
    first = cols_n * base
    for n in range(first + excess_max):
        meta[n] = -1
        pos[n] = 0
    for o in range(cols_n + 1):
        pos[first + excess_max + o] = 0

    def one(j, carry):
        t = ids_ref[j]
        owner = t & (cols_n - 1)
        r = pos[first + excess_max + owner]
        pos[first + excess_max + owner] = r + 1
        e = pos[first + excess_max + cols_n]
        over = (r >= base).astype(jnp.int32)
        pos[first + excess_max + cols_n] = e + over
        at = jnp.where(r >= base, first + e, owner * base + r)
        pos[at] = j
        meta[at] = t
        return carry

    lax.fori_loop(0, slots, one, 0)
    meta[first + excess_max] = pos[first + excess_max + cols_n]


def pack(tiles, ids, me, cols_n, base, excess_max, streams):
    slots = tiles.shape[0]
    count = LINES * base + 1
    first = cols_n * base

    n_out = 1 if streams else cols_n - 1

    def kernel(ids_ref, me_ref, tiles_ref, *rest):
        outs, (meta, held, pos, sems) = rest[:n_out], rest[n_out:]
        list_slots(ids_ref, pos, meta, slots, cols_n, base, excess_max)
        moves = []
        for n in range(count if streams else 0):
            at = n if n < LINES * base else first
            moves.append((meta[at] >= 0, pos[at], outs[0].at[n]))
        for k in range(1, 1 if streams else cols_n):
            owner = me_ref[0] ^ k
            for r in range(base):
                at = owner * base + r
                moves.append(((meta[at] >= 0) & (owner >= LINES), pos[at], outs[k - 1].at[r]))
        if streams:
            held = outs[0]
        for n, (cond, slot, _) in enumerate(moves):

            @pl.when(cond)
            def _(n=n, slot=slot):
                pltpu.make_async_copy(tiles_ref.at[slot], held.at[n], sems.at[0, n]).start()

        for n, (cond, slot, dst) in enumerate(moves):

            @pl.when(cond)
            def _(n=n, slot=slot, dst=dst):
                pltpu.make_async_copy(tiles_ref.at[slot], held.at[n], sems.at[0, n]).wait()
                if not streams:
                    pltpu.make_async_copy(held.at[n], dst, sems.at[1, n]).start()

        for n, (cond, _, dst) in enumerate([] if streams else moves):

            @pl.when(cond)
            def _(n=n, dst=dst):
                pltpu.make_async_copy(held.at[n], dst, sems.at[1, n]).wait()

    one = tiles.shape[1:]
    total = count if streams else (cols_n - 1) * base
    got = call(
        kernel,
        8,
        out_shape=tuple(
            pltpu.VMEM((count,) + one, F32) if streams else pltpu.HBM((base,) + one, F32) for _ in range(n_out)
        )
        + (jax.ShapeDtypeStruct((META,), jnp.int32),),
        in_specs=[SMEM, SMEM, HBM],
        out_specs=tuple(VMEM if streams else HBM for _ in range(n_out)) + (SMEM,),
        scratch_shapes=[
            pltpu.VMEM((total,) + one, F32),
            pltpu.SMEM((first + excess_max + cols_n + 1,), jnp.int32),
            pltpu.SemaphoreType.DMA((2, total)),
        ],
        name="pack_streams" if streams else "pack_shifts",
    )(ids, me, tiles)
    return got[:-1], got[-1]


def unwritten(shape):
    def kernel(out_ref):
        pass

    return call(kernel, 2, out_shape=jax.ShapeDtypeStruct(shape, F32), out_specs=HBM, name="unwritten")()


def extract(
    parts, origins, rest, near, ids, source_rows, me, odd, cols_n, base, tiles=None, arrived=(), arrived_from=()
):
    block = rest.shape[-1]
    bits = block.bit_length() - 1
    width = CBLK * cols_n
    width_bits, cols_bits = width.bit_length() - 1, cols_n.bit_length() - 1
    wide = 2 * CBLK
    own = tiles is not None
    count = LINES * base + 1
    depth = cols_n // LINES
    tiles_n = ids.shape[0]
    first = cols_n * base
    per = rest.shape[0] // cols_n

    def kernel(near_ref, ids_ref, rows_ref, me_ref, odd_ref, *rest_refs):
        part_refs, rest_refs = rest_refs[: len(parts)], rest_refs[len(parts) :]
        rest_ref, rest_refs = rest_refs[0], rest_refs[1:]
        if own:
            tiles_ref, arrived_refs = rest_refs[0], rest_refs[1 : 1 + len(arrived)]
        held_out, keep, send, top, held, sem, out_sem = rest_refs[-7:]
        me = me_ref[0]
        level, line = lax.shift_right_logical(me, 1), me & 1
        gathered = me < LINES

        def fetch(src, t, wanted):
            column = t & (width - 1)
            row = lax.shift_right_logical(t, width_bits)
            if own:
                ours = (column & (cols_n - 1)) == me
                place = row * CBLK + lax.shift_right_logical(column, cols_bits)
            else:
                ours = column < LINES
                place = row * CBLK + column

            @pl.when((t >= 0) & ours & wanted)
            def _():
                pltpu.make_async_copy(src, held.at[place], sem).start()

        if own:

            @pl.when(~gathered)
            def _():
                def one(j, carry):
                    fetch(tiles_ref.at[j], ids_ref[j], True)
                    return carry

                lax.fori_loop(0, tiles_n, one, 0)
                for ref, (k, pairs) in zip(arrived_refs, arrived_from):
                    here = functools.reduce(jnp.logical_or, [me == b for _, b in pairs])
                    for r in range(base):
                        fetch(ref.at[r], near_ref[k, me * base + r], here)

        for ref, (step, cross) in zip(part_refs, origins):
            if isinstance(step, tuple):
                by_level = step[0]
                for z in range(1, depth):
                    by_level = jnp.where(level == z, step[z], by_level)
                step = by_level
            at = level + step
            valid = (at >= 0) & (at < depth)
            source = at * LINES + (1 - line if cross else line)
            if own:
                valid = valid & (gathered | (source != me))

            @pl.when(valid)
            def _(ref=ref, source=source):
                k = source ^ me

                def streams():
                    for q in range(count - 1):
                        fetch(ref.at[q], near_ref[k, q], True)

                if own:
                    pl.when(gathered)(streams)
                else:
                    streams()
                fetch(ref.at[count - 1], near_ref[k, first], True)

        most = near_ref[0, first + per + 1]
        for k in range(1, cols_n):
            most = jnp.maximum(most, near_ref[k, first + per + 1])

        @pl.when(most > 1)
        def _():
            for k in range(cols_n):

                def one(e, carry, k=k):
                    fetch(rest_ref.at[k * per + e], near_ref[k, first + 1 + e], (gathered | (k > 0)) if own else True)
                    return carry

                lax.fori_loop(0, per, one, 0)

        pltpu.make_async_copy(held, held, sem).wait()
        copy_out = pltpu.make_async_copy(held, held_out, out_sem)
        copy_out.start()
        for m in range(CBLK):
            for c in range(2):
                top[2 * m + c] = held[m, c]
        for out, half in ((keep, odd_ref[0]), (send, 1 - odd_ref[0])):

            def pick(j, carry, out=out, half=half):
                row = rows_ref[half * block + j]
                here = row >= 0
                row = jnp.maximum(row, 0)
                tile = lax.shift_right_logical(row, bits) * CBLK
                inner = row & (block - 1)
                for m in range(CBLK):
                    for c in range(2):
                        value = held[tile + m, c, pl.ds(inner, 1), :]
                        out[2 * m + c, pl.ds(j, 1), :] = jnp.where(here, value, 0.0)
                return carry

            lax.fori_loop(0, block, pick, 0, unroll=8)
        copy_out.wait()

    part_rows = jax.ShapeDtypeStruct((wide, block, block), F32)
    operands = list(parts) + [rest] + ([tiles] + list(arrived) if own else [])
    operands = [pltpu.with_memory_space_constraint(x, pltpu.HBM) for x in operands]
    return call(
        kernel,
        12,
        out_shape=(pltpu.HBM((tiles_n, 2, block, block), F32), part_rows, part_rows, part_rows),
        in_specs=[SMEM] * 5 + [HBM] * len(operands),
        out_specs=(HBM, VMEM, VMEM, VMEM),
        scratch_shapes=[
            pltpu.VMEM((tiles_n, 2, block, block), F32),
            pltpu.SemaphoreType.DMA,
            pltpu.SemaphoreType.DMA,
        ],
        name="own_rows" if own else "panel_rows",
    )(near, ids, source_rows, me, odd, *operands)


def exchange(keep, send, top, far, my_row, rows_n, earlier=(), meanwhile=None):
    def cross(x, step):
        return lax.ppermute(x, "prow", [(p, p ^ step) for p in range(rows_n)])

    total = keep + cross(send, 1)
    if rows_n == 4:
        there = far[None, :, None]
        second = my_row >= 2
        message = jnp.where(there & ~second, top, total)
        message = lax.optimization_barrier((message, tuple(earlier)))[0]
        got = cross(message, 2)
        if meanwhile is not None:
            got = lax.optimization_barrier((got, meanwhile))[0]
        total = total + jnp.where(there & second, 0.0, got)
        held = jnp.where(second, got, top)
        return (total, cross(total, 1)), (held, cross(held, 1)), got
    held = top
    step = 2
    while step < rows_n:
        got = lax.ppermute(held, "prow", [(p, p + step) for p in range(step)])
        held = jnp.where((my_row >= step) & (my_row < 2 * step), got, held)
        total = total + cross(total, step)
        step *= 2
    return (total, cross(total, 1)), (held, cross(held, 1)), total


def fix_chained(chain_ref, new_ref, odd, old_refs, block):
    @pl.when(chain_ref[block] > 0)
    def _():
        def one(i, carry):
            j = chain_ref[i]

            @pl.when((j >= 0) & (odd == 0))
            def _():
                new_ref[1, :, pl.ds(i, 1), :] = old_refs[0][:, pl.ds(j, 1), :]

            @pl.when((j >= 0) & (odd == 1))
            def _():
                new_ref[1, :, pl.ds(i, 1), :] = old_refs[1][:, pl.ds(j, 1), :]

            return carry

        lax.fori_loop(0, block, one, 0)


def replace_rows(targets_ref, odd, old_refs, held, block):
    bits = block.bit_length() - 1

    spare = held.shape[0] - CBLK
    for ref, half in ((old_refs[0], odd), (old_refs[1], 1 - odd)):

        def one(j, carry, ref=ref, half=half):
            row = targets_ref[half * block + j]
            tile = jnp.where(row >= 0, lax.shift_right_logical(row, bits) * CBLK, spare)
            inner = row & (block - 1)
            for m in range(CBLK):
                for c in range(2):
                    held[tile + m, c, pl.ds(inner, 1), :] = ref[2 * m + c, pl.ds(j, 1), :]
            return carry

        lax.fori_loop(0, block, one, 0, unroll=8)


def split(x):
    high = x.astype(BF16)
    return high, (x - high.astype(F32)).astype(BF16)


def dot3(high, low, w_high, w_low):
    return (
        jnp.dot(high, w_high, preferred_element_type=F32)
        + jnp.dot(high, w_low, preferred_element_type=F32)
        + jnp.dot(low, w_high, preferred_element_type=F32)
    )


def store_complex(high_ref, low_ref, row, col, re, im):
    k, n = re.shape
    for r, c, value in ((0, 0, re), (0, 1, im), (1, 0, -im), (1, 1, re)):
        high, low = split(value)
        rows, cols = pl.ds(row + r * k, k), pl.ds(col + c * n, n)
        high_ref[rows, cols] = high
        low_ref[rows, cols] = low


def panel_factors(held, new, old, inverses, targets, chain, my_row, group):
    block = held.shape[-1]
    row_tiles = held.shape[0] // CBLK
    rows = row_tiles * block

    def kernel(tgt, chain_ref, row_ref, held_in, new_a, new_b, old_a, old_b, inv_ref, high_ref, low_ref, top_ref, *rest):
        held_ref, new_ref, i0h, i0l, i1h, i1l, uh, ul, sem = rest
        odd = lax.rem(row_ref[0], 2)
        copy = pltpu.make_async_copy(held_in, held_ref.at[: CBLK * row_tiles], sem)
        copy.start()
        new_ref[odd] = new_a[...]
        new_ref[1 - odd] = new_b[...]
        fix_chained(chain_ref, new_ref, odd, (old_a, old_b), block)
        store_complex(i0h, i0l, 0, 0, inv_ref[0, 0], inv_ref[0, 1])
        store_complex(i1h, i1l, 0, 0, inv_ref[1, 0], inv_ref[1, 1])
        store_complex(uh, ul, 0, 0, new_ref[0, 2], new_ref[0, 3])
        lower = dot3(
            *split(jnp.concatenate([new_ref[1, 0], new_ref[1, 1]], axis=1)), i0h[...], i0l[...]
        )
        top_ref[...] = lower
        copy.wait()
        replace_rows(tgt, odd, (old_a, old_b), held_ref, block)

        @pl.when(row_ref[0] == 1)
        def _():
            for m in range(CBLK):
                for c in range(2):
                    held_ref[m, c] = new_ref[1, 2 * m + c]

        def one(g, carry):
            x = [
                jnp.concatenate(
                    [
                        jnp.concatenate(
                            [held_ref[(g * group + t) * CBLK + m, 0], held_ref[(g * group + t) * CBLK + m, 1]], axis=1
                        )
                        for t in range(group)
                    ],
                    axis=0,
                )
                for m in range(CBLK)
            ]
            at = pl.ds(g * (group * block), group * block)
            l0h, l0l = split(dot3(*split(x[0]), i0h[...], i0l[...]))
            high_ref[at, : 2 * block] = l0h
            low_ref[at, : 2 * block] = l0l
            y = x[1] - dot3(l0h, l0l, uh[...], ul[...])
            l1h, l1l = split(dot3(*split(y), i1h[...], i1l[...]))
            high_ref[at, 2 * block :] = l1h
            low_ref[at, 2 * block :] = l1l
            return carry

        for g in range(row_tiles // group):
            one(g, 0)

    wide = pltpu.VMEM((2 * block, 2 * block), BF16)
    return call(
        kernel,
        20,
        out_shape=(
            jax.ShapeDtypeStruct((rows, 4 * block), BF16),
            jax.ShapeDtypeStruct((rows, 4 * block), BF16),
            jax.ShapeDtypeStruct((block, 2 * block), F32),
        ),
        in_specs=[SMEM, SMEM, SMEM, HBM] + [VMEM] * 5,
        out_specs=(VMEM, VMEM, VMEM),
        scratch_shapes=[pltpu.VMEM((held.shape[0] + CBLK,) + held.shape[1:], F32), pltpu.VMEM((2, 2 * CBLK, block, block), F32)]
        + [wide] * 6
        + [pltpu.SemaphoreType.DMA],
        name="panel_factors",
    )(targets, chain, my_row, pltpu.with_memory_space_constraint(held, pltpu.HBM), *new, *old, inverses)


def update(held, new, old, high, low, lower_top, targets, chain, my_row, my_col, rows_n, group):
    block = held.shape[-1]
    row_tiles = held.shape[0] // CBLK
    rows = row_tiles * block
    steps = row_tiles // group
    span = group * block

    def kernel(tgt, chain_ref, row_ref, col_ref, held_in, new_a, new_b, old_a, old_b, high_in, low_in, top_ref, out_ref, *rest):
        held_ref, new_ref, high_ref, low_ref, res_ref, wh, wl, sem, in_sems, out_sems = rest
        odd = lax.rem(row_ref[0], 2)
        copy = pltpu.make_async_copy(held_in, held_ref.at[: CBLK * row_tiles], sem)
        copy.start()
        for g in range(steps):
            at = pl.ds(g * span, span)
            for n, (src, dst) in enumerate(((high_in, high_ref), (low_in, low_ref))):
                pltpu.make_async_copy(src.at[at], dst.at[at], in_sems.at[2 * g + n]).start()
        new_ref[odd] = new_a[...]
        new_ref[1 - odd] = new_b[...]
        fix_chained(chain_ref, new_ref, odd, (old_a, old_b), block)
        for m in range(CBLK):
            store_complex(wh, wl, 0, 2 * m * block, new_ref[0, 2 * m], new_ref[0, 2 * m + 1])
        first = dot3(*split(top_ref[...]), wh[: 2 * block, :], wl[: 2 * block, :])
        second = []
        for n in range(2 * CBLK):
            second.append(new_ref[1, n] - first[:, n * block : (n + 1) * block])
            new_ref[1, n] = second[n]
        for m in range(CBLK):
            store_complex(wh, wl, 2 * block, 2 * m * block, second[2 * m], second[2 * m + 1])
        copy.wait()
        replace_rows(tgt, odd, (old_a, old_b), held_ref, block)
        for g in range(steps):
            at = pl.ds(g * span, span)
            for n, (src, dst) in enumerate(((high_in, high_ref), (low_in, low_ref))):
                pltpu.make_async_copy(src.at[at], dst.at[at], in_sems.at[2 * g + n]).wait()
            y = dot3(high_ref[at, :], low_ref[at, :], wh[...], wl[...])
            for t in range(group):
                tile = g * group + t
                for m in range(CBLK):
                    for c in range(2):
                        n = 2 * m + c
                        res_ref[c, tile * block : (tile + 1) * block, m * block : (m + 1) * block] = (
                            held_ref[tile * CBLK + m, c]
                            - y[t * block : (t + 1) * block, n * block : (n + 1) * block]
                        )
            for panel in range(2):

                @pl.when(col_ref[0] == panel)
                def _(panel=panel, at=at):
                    for c in range(2):
                        cols = slice((2 * panel + c) * block, (2 * panel + c + 1) * block)
                        res_ref[c, at, :block] = high_ref[at, cols].astype(F32) + low_ref[at, cols].astype(F32)

            if g == 0:
                for p in range(2):

                    @pl.when(row_ref[0] == p)
                    def _(p=p):
                        for c in range(2):
                            for m in range(CBLK):
                                res_ref[c, :block, m * block : (m + 1) * block] = new_ref[p, 2 * m + c]

                @pl.when((row_ref[0] == 1) & (col_ref[0] == 0))
                def _():
                    for c in range(2):
                        res_ref[c, :block, :block] = top_ref[:, c * block : (c + 1) * block]

            for c in range(2):
                pltpu.make_async_copy(res_ref.at[c, at], out_ref.at[c, at], out_sems.at[2 * g + c]).start()
        for g in range(steps):
            at = pl.ds(g * span, span)
            for c in range(2):
                pltpu.make_async_copy(res_ref.at[c, at], out_ref.at[c, at], out_sems.at[2 * g + c]).wait()

    return call(
        kernel,
        24,
        out_shape=jax.ShapeDtypeStruct((2, rows, CBLK * block), F32),
        in_specs=[SMEM] * 4 + [HBM] + [VMEM] * 4 + [ANY] * 2 + [VMEM],
        out_specs=ANY,
        scratch_shapes=[
            pltpu.VMEM((held.shape[0] + CBLK,) + held.shape[1:], F32),
            pltpu.VMEM((2, 2 * CBLK, block, block), F32),
            pltpu.VMEM((rows, 4 * block), BF16),
            pltpu.VMEM((rows, 4 * block), BF16),
            pltpu.VMEM((2, rows, CBLK * block), F32),
            pltpu.VMEM((4 * block, 4 * block), BF16),
            pltpu.VMEM((4 * block, 4 * block), BF16),
            pltpu.SemaphoreType.DMA,
            pltpu.SemaphoreType.DMA((2 * steps,)),
            pltpu.SemaphoreType.DMA((2 * steps,)),
        ],
        name="update",
    )(
        targets, chain, my_row, my_col, pltpu.with_memory_space_constraint(held, pltpu.HBM), *new, *old, high, low, lower_top
    )


def per_device(assembly, slot_tile, pivots, inverses):
    cols_n = lax.axis_size("pcol")
    rows_n = lax.axis_size("prow")
    my_col = lax.axis_index("pcol")
    my_row = lax.axis_index("prow")
    tiles = assembly[0]
    slots = tiles.shape[0]
    block = tiles.shape[-1]
    row_tiles = slots // CBLK
    base = (slots + cols_n - 1) // cols_n
    excess_max = slots // (base + 1)
    depth = cols_n // LINES
    group = 4 if row_tiles % 4 == 0 else 1
    level = my_col // LINES
    me = my_col.astype(jnp.int32).reshape(1)
    me_row = my_row.astype(jnp.int32).reshape(1)
    odd = me_row % 2
    ids = slot_tile[0]

    picks = jnp.arange(2 * block, dtype=jnp.int32)
    first, second = pivots[0], pivots[1]
    same = (second[:, None] == first[None, :]) & (first[None, :] >= 2 * block)
    chained = jnp.sum(jnp.where(same, picks[None, :block], 0), axis=1)
    second_source = jnp.where(jnp.any(same, axis=1), chained, second)
    replaced = jnp.any(same, axis=0)
    wanted = jnp.concatenate([first, second_source])
    named = jnp.concatenate([first, second])
    moved = (named != picks) & ~jnp.concatenate([replaced, jnp.zeros_like(replaced)])

    def local_row(row, keep):
        ours = (row // block % rows_n == my_row) & keep
        return jnp.where(ours, row // block // rows_n * block + row % block, -1)

    source_rows = local_row(wanted, True)
    targets = local_row(named, moved)
    away = named // block % rows_n >= 2
    far = jnp.where(my_row % 2 == 0, away[:block], away[block:])
    fix = jnp.any(same, axis=1) & away[block:] & (my_row >= 2) & (rows_n == 4)
    chain = jnp.concatenate([jnp.where(fix, chained, -1), jnp.sum(fix.astype(jnp.int32))[None]])

    def after(values, earlier):
        return lax.optimization_barrier((tuple(values), tuple(earlier)))[0]

    def swapped(phase):
        due = []
        for z in range(depth):
            chunks = []
            for t in range(1, depth):
                chunks += [("up", t)] * (z - t >= 0) + [("down", t)] * (z + t < depth)
            due.append(chunks[phase - 2])
        return due

    def shift_pairs(k, phase):
        zm, dx = k // LINES, k % LINES
        pairs = []
        for i in range(cols_n):
            if dx == 0 and zm >= 2 and (i ^ k) // LINES < depth - 1:
                due = depth - 1
            elif zm == depth - 1 or (dx == 0 and zm == 1):
                due = depth
            else:
                due = depth + 1
            if (i ^ k) >= LINES and due == phase:
                pairs.append((i, i ^ k))
        return pairs

    def after(values, earlier):
        return lax.optimization_barrier((tuple(values), tuple(earlier)))[0]

    (packed,), meta = pack(tiles, ids, me, cols_n, base, excess_max, True)
    shifted, _ = pack(tiles, after([ids], [packed])[0], me, cols_n, base, excess_max, False)
    parts, origins = [packed], [(0, False)]
    chunk = {("up", 0): packed, ("down", 0): packed}
    arrived, arrived_from = [], []
    done, work = [], []
    near = meta[None]
    for phase in range(1, depth + 2):
        last, work = work, []
        if phase < depth:
            t = phase
            up = [(i, i + LINES) for i in range((t - 1) * LINES, cols_n - LINES)]
            down = [(i, i - LINES) for i in range(LINES, cols_n - (t - 1) * LINES)]
            work.append((chunk["up", t - 1], up, ("up", t), (-t, False)))
            work.append((chunk["down", t - 1], down, ("down", t), (t, False)))
        if phase == 1:
            work.append((packed, [(i, i ^ 1) for i in range(cols_n)], None, (0, True)))
        elif phase <= depth:
            due = swapped(phase)
            keys = sorted(set(due))
            if len(keys) <= 2:
                for key in keys:
                    levels = [z for z in range(depth) if due[z] == key]
                    pairs = [(i, i ^ 1) for z in levels for i in range(z * LINES, (z + 1) * LINES)]
                    steps = tuple(
                        (-key[1] if key[0] == "up" else key[1]) if z in levels else depth for z in range(depth)
                    )
                    work.append((chunk[key], pairs, None, (steps, True)))
            else:
                x = chunk[due[0]]
                for key in keys:
                    if key != due[0]:
                        levels = [level == z for z in range(depth) if due[z] == key]
                        x = jnp.where(functools.reduce(jnp.logical_or, levels), chunk[key], x)
                steps = tuple(-t if d == "up" else t for d, t in due)
                work.append((x, [(i, i ^ 1) for i in range(cols_n)], None, (steps, True)))
        else:
            gathered_all = [got for got, w in zip(done, last) if not isinstance(w[2], int)]
            shifted_first = [got for got, w in zip(done, last) if isinstance(w[2], int)]
        for k in reversed(range(1, cols_n)):
            pairs = shift_pairs(k, phase)
            if pairs:
                work.append((shifted[k - 1], pairs, k, pairs))
        before = done
        values = after([w[0] for w in work], done) if done else [w[0] for w in work]
        done = [lax.ppermute(x, "pcol", w[1]) for x, w in zip(values, work)]
        for got, (_, _, key, origin) in zip(done, work):
            if isinstance(key, int):
                arrived.append(got)
                arrived_from.append((key, origin))
            else:
                parts.append(got)
                origins.append(origin)
                if key is not None:
                    chunk[key] = got
        step = 1 << (phase - 1)
        if step < cols_n:
            if phase > 1:
                near = after([near], before)[0]
            got = lax.ppermute(near, "pcol", [(i, i ^ step) for i in range(cols_n)])
            near = jnp.concatenate([near, got])
            done = done + [got]
        if phase == 1:
            done = done + [source_rows, targets, far, chain]
    most = jnp.max(near[:, cols_n * base + excess_max])

    def gather_rest():
        mine = meta[cols_n * base + 1 : cols_n * base + excess_max]
        slot = jnp.sum(
            jnp.where(mine[:, None] == ids[None, :], jnp.arange(slots, dtype=jnp.int32)[None, :], 0), axis=1
        )
        rest = jnp.stack(
            [lax.dynamic_index_in_dim(tiles, slot[e], 0, False) for e in range(excess_max - 1)]
        )
        others = [
            lax.ppermute(rest, "pcol", [(i, i ^ k) for i in range(cols_n)]) for k in range(1, cols_n)
        ]
        return jnp.concatenate([rest] + others)

    def no_rest():
        return unwritten((cols_n * (excess_max - 1),) + tiles.shape[1:])

    rest = lax.cond(most > 1, gather_rest, no_rest)

    late_rows = after([source_rows], gathered_all)[0]
    held_p, keep_p, send_p, top_p = extract(
        parts, origins, rest, near, ids, late_rows, me, odd, cols_n, base
    )
    new_p, old_p, crossed = exchange(keep_p, send_p, top_p, far, my_row, rows_n, shifted_first)
    high, low, lower_top = panel_factors(held_p, new_p, old_p, inverses, targets, chain, me_row, group)

    late_rows = after([source_rows], [crossed])[0]
    held, keep, send, top = extract(
        parts, origins, rest, near, ids, late_rows, me, odd, cols_n, base, tiles, arrived, arrived_from
    )
    new, old, _ = exchange(keep, send, top, far, my_row, rows_n, meanwhile=high)
    return update(held, new, old, high, low, lower_top, targets, chain, me_row, me, rows_n, group)


def solution(mesh):
    in_specs = (P("prow", "pcol", None, None, None), P("prow", "pcol"), P(), P())
    out_specs = P(None, "prow", "pcol")
    return jax.shard_map(
        per_device, mesh=mesh, in_specs=in_specs, out_specs=out_specs, check_vma=False
    )
```

```python
import functools

import jax
import jax.numpy as jnp
from jax import lax
from jax.experimental import pallas as pl
from jax.experimental.pallas import tpu as pltpu
from jax.sharding import PartitionSpec as P

CBLK = 2
LINES = 2
F32 = jnp.float32
BF16 = jnp.bfloat16
MIB = 1024 * 1024
META = 128

ANY = pl.BlockSpec(memory_space=pl.ANY)
SMEM = pl.BlockSpec(memory_space=pltpu.SMEM)
VMEM = pl.BlockSpec(memory_space=pltpu.VMEM)
HBM = pl.BlockSpec(memory_space=pltpu.HBM)


def call(kernel, mib, **kw):
    return pl.pallas_call(
        kernel,
        compiler_params=pltpu.CompilerParams(vmem_limit_bytes=mib * MIB),
        cost_estimate=pl.CostEstimate(flops=0, bytes_accessed=0, transcendentals=0),
        **kw,
    )


def list_slots(ids_ref, pos, meta, slots, cols_n, base, excess_max):
    first = cols_n * base
    for n in range(first + excess_max):
        meta[n] = -1
        pos[n] = 0
    for o in range(cols_n + 1):
        pos[first + excess_max + o] = 0

    def one(j, carry):
        t = ids_ref[j]
        owner = t & (cols_n - 1)
        r = pos[first + excess_max + owner]
        pos[first + excess_max + owner] = r + 1
        e = pos[first + excess_max + cols_n]
        over = (r >= base).astype(jnp.int32)
        pos[first + excess_max + cols_n] = e + over
        at = jnp.where(r >= base, first + e, owner * base + r)
        pos[at] = j
        meta[at] = t
        return carry

    lax.fori_loop(0, slots, one, 0)
    meta[first + excess_max] = pos[first + excess_max + cols_n]


def pack(tiles, ids, me, cols_n, base, excess_max, streams):
    slots = tiles.shape[0]
    count = LINES * base + 1
    first = cols_n * base

    n_out = 1 if streams else cols_n - 1

    def kernel(ids_ref, me_ref, tiles_ref, *rest):
        outs, (meta, held, pos, sems) = rest[:n_out], rest[n_out:]
        list_slots(ids_ref, pos, meta, slots, cols_n, base, excess_max)
        moves = []
        for n in range(count if streams else 0):
            at = n if n < LINES * base else first
            moves.append((meta[at] >= 0, pos[at], outs[0].at[n]))
        for k in range(1, 1 if streams else cols_n):
            owner = me_ref[0] ^ k
            for r in range(base):
                at = owner * base + r
                moves.append(((meta[at] >= 0) & (owner >= LINES), pos[at], outs[k - 1].at[r]))
        if streams:
            held = outs[0]
        for n, (cond, slot, _) in enumerate(moves):

            @pl.when(cond)
            def _(n=n, slot=slot):
                pltpu.make_async_copy(tiles_ref.at[slot], held.at[n], sems.at[0, n]).start()

        for n, (cond, slot, dst) in enumerate(moves):

            @pl.when(cond)
            def _(n=n, slot=slot, dst=dst):
                pltpu.make_async_copy(tiles_ref.at[slot], held.at[n], sems.at[0, n]).wait()
                if not streams:
                    pltpu.make_async_copy(held.at[n], dst, sems.at[1, n]).start()

        for n, (cond, _, dst) in enumerate([] if streams else moves):

            @pl.when(cond)
            def _(n=n, dst=dst):
                pltpu.make_async_copy(held.at[n], dst, sems.at[1, n]).wait()

    one = tiles.shape[1:]
    total = count if streams else (cols_n - 1) * base
    got = call(
        kernel,
        8,
        out_shape=tuple(
            pltpu.VMEM((count,) + one, F32) if streams else pltpu.HBM((base,) + one, F32) for _ in range(n_out)
        )
        + (jax.ShapeDtypeStruct((META,), jnp.int32),),
        in_specs=[SMEM, SMEM, HBM],
        out_specs=tuple(VMEM if streams else HBM for _ in range(n_out)) + (SMEM,),
        scratch_shapes=[
            pltpu.VMEM((total,) + one, F32),
            pltpu.SMEM((first + excess_max + cols_n + 1,), jnp.int32),
            pltpu.SemaphoreType.DMA((2, total)),
        ],
        name="pack_streams" if streams else "pack_shifts",
    )(ids, me, tiles)
    return got[:-1], got[-1]


def unwritten(shape):
    def kernel(out_ref):
        pass

    return call(kernel, 2, out_shape=jax.ShapeDtypeStruct(shape, F32), out_specs=HBM, name="unwritten")()


def extract(
    parts, origins, rest, near, ids, source_rows, me, odd, cols_n, base, tiles=None, arrived=(), arrived_from=()
):
    block = rest.shape[-1]
    bits = block.bit_length() - 1
    width = CBLK * cols_n
    width_bits, cols_bits = width.bit_length() - 1, cols_n.bit_length() - 1
    wide = 2 * CBLK
    own = tiles is not None
    count = LINES * base + 1
    depth = cols_n // LINES
    tiles_n = ids.shape[0]
    first = cols_n * base
    per = rest.shape[0] // cols_n

    def kernel(near_ref, ids_ref, rows_ref, me_ref, odd_ref, *rest_refs):
        part_refs, rest_refs = rest_refs[: len(parts)], rest_refs[len(parts) :]
        rest_ref, rest_refs = rest_refs[0], rest_refs[1:]
        if own:
            tiles_ref, arrived_refs = rest_refs[0], rest_refs[1 : 1 + len(arrived)]
        held_out, keep, send, top, held, sem, out_sem = rest_refs[-7:]
        me = me_ref[0]
        level, line = lax.shift_right_logical(me, 1), me & 1
        gathered = me < LINES

        def fetch(src, t, wanted):
            column = t & (width - 1)
            row = lax.shift_right_logical(t, width_bits)
            if own:
                ours = (column & (cols_n - 1)) == me
                place = row * CBLK + lax.shift_right_logical(column, cols_bits)
            else:
                ours = column < LINES
                place = row * CBLK + column

            @pl.when((t >= 0) & ours & wanted)
            def _():
                pltpu.make_async_copy(src, held.at[place], sem).start()

        if own:

            @pl.when(~gathered)
            def _():
                def one(j, carry):
                    fetch(tiles_ref.at[j], ids_ref[j], True)
                    return carry

                lax.fori_loop(0, tiles_n, one, 0)
                for ref, (k, pairs) in zip(arrived_refs, arrived_from):
                    here = functools.reduce(jnp.logical_or, [me == b for _, b in pairs])
                    for r in range(base):
                        fetch(ref.at[r], near_ref[k, me * base + r], here)

        for ref, (step, cross) in zip(part_refs, origins):
            if isinstance(step, tuple):
                by_level = step[0]
                for z in range(1, depth):
                    by_level = jnp.where(level == z, step[z], by_level)
                step = by_level
            at = level + step
            valid = (at >= 0) & (at < depth)
            source = at * LINES + (1 - line if cross else line)
            if own:
                valid = valid & (gathered | (source != me))

            @pl.when(valid)
            def _(ref=ref, source=source):
                k = source ^ me

                def streams():
                    for q in range(count - 1):
                        fetch(ref.at[q], near_ref[k, q], True)

                if own:
                    pl.when(gathered)(streams)
                else:
                    streams()
                fetch(ref.at[count - 1], near_ref[k, first], True)

        most = near_ref[0, first + per + 1]
        for k in range(1, cols_n):
            most = jnp.maximum(most, near_ref[k, first + per + 1])

        @pl.when(most > 1)
        def _():
            for k in range(cols_n):

                def one(e, carry, k=k):
                    fetch(rest_ref.at[k * per + e], near_ref[k, first + 1 + e], (gathered | (k > 0)) if own else True)
                    return carry

                lax.fori_loop(0, per, one, 0)

        pltpu.make_async_copy(held, held, sem).wait()
        copy_out = pltpu.make_async_copy(held, held_out, out_sem)
        copy_out.start()
        for m in range(CBLK):
            for c in range(2):
                top[2 * m + c] = held[m, c]
        for out, half in ((keep, odd_ref[0]), (send, 1 - odd_ref[0])):

            def pick(j, carry, out=out, half=half):
                row = rows_ref[half * block + j]
                here = row >= 0
                row = jnp.maximum(row, 0)
                tile = lax.shift_right_logical(row, bits) * CBLK
                inner = row & (block - 1)
                for m in range(CBLK):
                    for c in range(2):
                        value = held[tile + m, c, pl.ds(inner, 1), :]
                        out[2 * m + c, pl.ds(j, 1), :] = jnp.where(here, value, 0.0)
                return carry

            lax.fori_loop(0, block, pick, 0, unroll=8)
        copy_out.wait()

    part_rows = jax.ShapeDtypeStruct((wide, block, block), F32)
    operands = list(parts) + [rest] + ([tiles] + list(arrived) if own else [])
    operands = [pltpu.with_memory_space_constraint(x, pltpu.HBM) for x in operands]
    return call(
        kernel,
        12,
        out_shape=(pltpu.HBM((tiles_n, 2, block, block), F32), part_rows, part_rows, part_rows),
        in_specs=[SMEM] * 5 + [HBM] * len(operands),
        out_specs=(HBM, VMEM, VMEM, VMEM),
        scratch_shapes=[
            pltpu.VMEM((tiles_n, 2, block, block), F32),
            pltpu.SemaphoreType.DMA,
            pltpu.SemaphoreType.DMA,
        ],
        name="own_rows" if own else "panel_rows",
    )(near, ids, source_rows, me, odd, *operands)


def exchange(keep, send, top, far, my_row, rows_n, earlier=(), meanwhile=None):
    def cross(x, step):
        return lax.ppermute(x, "prow", [(p, p ^ step) for p in range(rows_n)])

    total = keep + cross(send, 1)
    if rows_n == 4:
        there = far[None, :, None]
        second = my_row >= 2
        message = jnp.where(there & ~second, top, total)
        message = lax.optimization_barrier((message, tuple(earlier)))[0]
        got = cross(message, 2)
        if meanwhile is not None:
            got = lax.optimization_barrier((got, meanwhile))[0]
        total = total + jnp.where(there & second, 0.0, got)
        held = jnp.where(second, got, top)
        return (total, cross(total, 1)), (held, cross(held, 1)), got
    held = top
    step = 2
    while step < rows_n:
        got = lax.ppermute(held, "prow", [(p, p + step) for p in range(step)])
        held = jnp.where((my_row >= step) & (my_row < 2 * step), got, held)
        total = total + cross(total, step)
        step *= 2
    return (total, cross(total, 1)), (held, cross(held, 1)), total


def fix_chained(chain_ref, new_ref, odd, old_refs, block):
    @pl.when(chain_ref[block] > 0)
    def _():
        def one(i, carry):
            j = chain_ref[i]

            @pl.when((j >= 0) & (odd == 0))
            def _():
                new_ref[1, :, pl.ds(i, 1), :] = old_refs[0][:, pl.ds(j, 1), :]

            @pl.when((j >= 0) & (odd == 1))
            def _():
                new_ref[1, :, pl.ds(i, 1), :] = old_refs[1][:, pl.ds(j, 1), :]

            return carry

        lax.fori_loop(0, block, one, 0)


def replace_rows(targets_ref, odd, old_refs, held, block):
    bits = block.bit_length() - 1

    spare = held.shape[0] - CBLK
    for ref, half in ((old_refs[0], odd), (old_refs[1], 1 - odd)):

        def one(j, carry, ref=ref, half=half):
            row = targets_ref[half * block + j]
            tile = jnp.where(row >= 0, lax.shift_right_logical(row, bits) * CBLK, spare)
            inner = row & (block - 1)
            for m in range(CBLK):
                for c in range(2):
                    held[tile + m, c, pl.ds(inner, 1), :] = ref[2 * m + c, pl.ds(j, 1), :]
            return carry

        lax.fori_loop(0, block, one, 0, unroll=8)


def split(x):
    high = x.astype(BF16)
    return high, (x - high.astype(F32)).astype(BF16)


def dot3(high, low, w_high, w_low):
    return (
        jnp.dot(high, w_high, preferred_element_type=F32)
        + jnp.dot(high, w_low, preferred_element_type=F32)
        + jnp.dot(low, w_high, preferred_element_type=F32)
    )


def store_complex(high_ref, low_ref, row, col, re, im):
    k, n = re.shape
    for r, c, value in ((0, 0, re), (0, 1, im), (1, 0, -im), (1, 1, re)):
        high, low = split(value)
        rows, cols = pl.ds(row + r * k, k), pl.ds(col + c * n, n)
        high_ref[rows, cols] = high
        low_ref[rows, cols] = low


def panel_factors(held, new, old, inverses, targets, chain, my_row, group):
    block = held.shape[-1]
    row_tiles = held.shape[0] // CBLK
    rows = row_tiles * block

    def kernel(tgt, chain_ref, row_ref, held_in, new_a, new_b, old_a, old_b, inv_ref, high_ref, low_ref, top_ref, *rest):
        held_ref, new_ref, i0h, i0l, i1h, i1l, uh, ul, sem = rest
        odd = lax.rem(row_ref[0], 2)
        copy = pltpu.make_async_copy(held_in, held_ref.at[: CBLK * row_tiles], sem)
        copy.start()
        new_ref[odd] = new_a[...]
        new_ref[1 - odd] = new_b[...]
        fix_chained(chain_ref, new_ref, odd, (old_a, old_b), block)
        store_complex(i0h, i0l, 0, 0, inv_ref[0, 0], inv_ref[0, 1])
        store_complex(i1h, i1l, 0, 0, inv_ref[1, 0], inv_ref[1, 1])
        store_complex(uh, ul, 0, 0, new_ref[0, 2], new_ref[0, 3])
        lower = dot3(
            *split(jnp.concatenate([new_ref[1, 0], new_ref[1, 1]], axis=1)), i0h[...], i0l[...]
        )
        top_ref[...] = lower
        copy.wait()
        replace_rows(tgt, odd, (old_a, old_b), held_ref, block)

        @pl.when(row_ref[0] == 1)
        def _():
            for m in range(CBLK):
                for c in range(2):
                    held_ref[m, c] = new_ref[1, 2 * m + c]

        def one(g, carry):
            x = [
                jnp.concatenate(
                    [
                        jnp.concatenate(
                            [held_ref[(g * group + t) * CBLK + m, 0], held_ref[(g * group + t) * CBLK + m, 1]], axis=1
                        )
                        for t in range(group)
                    ],
                    axis=0,
                )
                for m in range(CBLK)
            ]
            at = pl.ds(g * (group * block), group * block)
            l0h, l0l = split(dot3(*split(x[0]), i0h[...], i0l[...]))
            high_ref[at, : 2 * block] = l0h
            low_ref[at, : 2 * block] = l0l
            y = x[1] - dot3(l0h, l0l, uh[...], ul[...])
            l1h, l1l = split(dot3(*split(y), i1h[...], i1l[...]))
            high_ref[at, 2 * block :] = l1h
            low_ref[at, 2 * block :] = l1l
            return carry

        for g in range(row_tiles // group):
            one(g, 0)

    wide = pltpu.VMEM((2 * block, 2 * block), BF16)
    return call(
        kernel,
        20,
        out_shape=(
            jax.ShapeDtypeStruct((rows, 4 * block), BF16),
            jax.ShapeDtypeStruct((rows, 4 * block), BF16),
            jax.ShapeDtypeStruct((block, 2 * block), F32),
        ),
        in_specs=[SMEM, SMEM, SMEM, HBM] + [VMEM] * 5,
        out_specs=(VMEM, VMEM, VMEM),
        scratch_shapes=[pltpu.VMEM((held.shape[0] + CBLK,) + held.shape[1:], F32), pltpu.VMEM((2, 2 * CBLK, block, block), F32)]
        + [wide] * 6
        + [pltpu.SemaphoreType.DMA],
        name="panel_factors",
    )(targets, chain, my_row, pltpu.with_memory_space_constraint(held, pltpu.HBM), *new, *old, inverses)


def update(held, new, old, high, low, lower_top, targets, chain, my_row, my_col, rows_n, group):
    block = held.shape[-1]
    row_tiles = held.shape[0] // CBLK
    rows = row_tiles * block
    steps = row_tiles // group
    span = group * block

    def kernel(tgt, chain_ref, row_ref, col_ref, held_in, new_a, new_b, old_a, old_b, high_ref, low_ref, top_ref, out_ref, *rest):
        held_ref, new_ref, res_ref, wh, wl, sem, out_sems = rest
        odd = lax.rem(row_ref[0], 2)
        copy = pltpu.make_async_copy(held_in, held_ref.at[: CBLK * row_tiles], sem)
        copy.start()
        new_ref[odd] = new_a[...]
        new_ref[1 - odd] = new_b[...]
        fix_chained(chain_ref, new_ref, odd, (old_a, old_b), block)
        for m in range(CBLK):
            store_complex(wh, wl, 0, 2 * m * block, new_ref[0, 2 * m], new_ref[0, 2 * m + 1])
        first = dot3(*split(top_ref[...]), wh[: 2 * block, :], wl[: 2 * block, :])
        second = []
        for n in range(2 * CBLK):
            second.append(new_ref[1, n] - first[:, n * block : (n + 1) * block])
            new_ref[1, n] = second[n]
        for m in range(CBLK):
            store_complex(wh, wl, 2 * block, 2 * m * block, second[2 * m], second[2 * m + 1])
        copy.wait()
        replace_rows(tgt, odd, (old_a, old_b), held_ref, block)
        for g in range(steps):
            at = pl.ds(g * span, span)
            y = dot3(high_ref[at, :], low_ref[at, :], wh[...], wl[...])
            for t in range(group):
                tile = g * group + t
                for m in range(CBLK):
                    for c in range(2):
                        n = 2 * m + c
                        res_ref[c, tile * block : (tile + 1) * block, m * block : (m + 1) * block] = (
                            held_ref[tile * CBLK + m, c]
                            - y[t * block : (t + 1) * block, n * block : (n + 1) * block]
                        )
            for panel in range(2):

                @pl.when(col_ref[0] == panel)
                def _(panel=panel, at=at):
                    for c in range(2):
                        cols = slice((2 * panel + c) * block, (2 * panel + c + 1) * block)
                        res_ref[c, at, :block] = high_ref[at, cols].astype(F32) + low_ref[at, cols].astype(F32)

            if g == 0:
                for p in range(2):

                    @pl.when(row_ref[0] == p)
                    def _(p=p):
                        for c in range(2):
                            for m in range(CBLK):
                                res_ref[c, :block, m * block : (m + 1) * block] = new_ref[p, 2 * m + c]

                @pl.when((row_ref[0] == 1) & (col_ref[0] == 0))
                def _():
                    for c in range(2):
                        res_ref[c, :block, :block] = top_ref[:, c * block : (c + 1) * block]

            for c in range(2):
                pltpu.make_async_copy(res_ref.at[c, at], out_ref.at[c, at], out_sems.at[2 * g + c]).start()
        for g in range(steps):
            at = pl.ds(g * span, span)
            for c in range(2):
                pltpu.make_async_copy(res_ref.at[c, at], out_ref.at[c, at], out_sems.at[2 * g + c]).wait()

    return call(
        kernel,
        24,
        out_shape=jax.ShapeDtypeStruct((2, rows, CBLK * block), F32),
        in_specs=[SMEM] * 4 + [HBM] + [VMEM] * 7,
        out_specs=ANY,
        scratch_shapes=[
            pltpu.VMEM((held.shape[0] + CBLK,) + held.shape[1:], F32),
            pltpu.VMEM((2, 2 * CBLK, block, block), F32),
            pltpu.VMEM((2, rows, CBLK * block), F32),
            pltpu.VMEM((4 * block, 4 * block), BF16),
            pltpu.VMEM((4 * block, 4 * block), BF16),
            pltpu.SemaphoreType.DMA,
            pltpu.SemaphoreType.DMA((2 * steps,)),
        ],
        name="update",
    )(
        targets, chain, my_row, my_col, pltpu.with_memory_space_constraint(held, pltpu.HBM), *new, *old, high, low, lower_top
    )


def per_device(assembly, slot_tile, pivots, inverses):
    cols_n = lax.axis_size("pcol")
    rows_n = lax.axis_size("prow")
    my_col = lax.axis_index("pcol")
    my_row = lax.axis_index("prow")
    tiles = assembly[0]
    slots = tiles.shape[0]
    block = tiles.shape[-1]
    row_tiles = slots // CBLK
    base = (slots + cols_n - 1) // cols_n
    excess_max = slots // (base + 1)
    depth = cols_n // LINES
    group = 4 if row_tiles % 4 == 0 else 1
    level = my_col // LINES
    me = my_col.astype(jnp.int32).reshape(1)
    me_row = my_row.astype(jnp.int32).reshape(1)
    odd = me_row % 2
    ids = slot_tile[0]

    picks = jnp.arange(2 * block, dtype=jnp.int32)
    first, second = pivots[0], pivots[1]
    same = (second[:, None] == first[None, :]) & (first[None, :] >= 2 * block)
    chained = jnp.sum(jnp.where(same, picks[None, :block], 0), axis=1)
    second_source = jnp.where(jnp.any(same, axis=1), chained, second)
    replaced = jnp.any(same, axis=0)
    wanted = jnp.concatenate([first, second_source])
    named = jnp.concatenate([first, second])
    moved = (named != picks) & ~jnp.concatenate([replaced, jnp.zeros_like(replaced)])

    def local_row(row, keep):
        ours = (row // block % rows_n == my_row) & keep
        return jnp.where(ours, row // block // rows_n * block + row % block, -1)

    source_rows = local_row(wanted, True)
    targets = local_row(named, moved)
    away = named // block % rows_n >= 2
    far = jnp.where(my_row % 2 == 0, away[:block], away[block:])
    fix = jnp.any(same, axis=1) & away[block:] & (my_row >= 2) & (rows_n == 4)
    chain = jnp.concatenate([jnp.where(fix, chained, -1), jnp.sum(fix.astype(jnp.int32))[None]])

    def after(values, earlier):
        return lax.optimization_barrier((tuple(values), tuple(earlier)))[0]

    def swapped(phase):
        due = []
        for z in range(depth):
            chunks = []
            for t in range(1, depth):
                chunks += [("up", t)] * (z - t >= 0) + [("down", t)] * (z + t < depth)
            due.append(chunks[phase - 2])
        return due

    def shift_pairs(k, phase):
        zm, dx = k // LINES, k % LINES
        pairs = []
        for i in range(cols_n):
            if dx == 0 and zm >= 2 and (i ^ k) // LINES < depth - 1:
                due = depth - 1
            elif zm == depth - 1 or (dx == 0 and zm == 1):
                due = depth
            else:
                due = depth + 1
            if (i ^ k) >= LINES and due == phase:
                pairs.append((i, i ^ k))
        return pairs

    def after(values, earlier):
        return lax.optimization_barrier((tuple(values), tuple(earlier)))[0]

    (packed,), meta = pack(tiles, ids, me, cols_n, base, excess_max, True)
    shifted, _ = pack(tiles, after([ids], [packed])[0], me, cols_n, base, excess_max, False)
    parts, origins = [packed], [(0, False)]
    chunk = {("up", 0): packed, ("down", 0): packed}
    arrived, arrived_from = [], []
    done, work = [], []
    near = meta[None]
    for phase in range(1, depth + 2):
        last, work = work, []
        if phase < depth:
            t = phase
            up = [(i, i + LINES) for i in range((t - 1) * LINES, cols_n - LINES)]
            down = [(i, i - LINES) for i in range(LINES, cols_n - (t - 1) * LINES)]
            work.append((chunk["up", t - 1], up, ("up", t), (-t, False)))
            work.append((chunk["down", t - 1], down, ("down", t), (t, False)))
        if phase == 1:
            work.append((packed, [(i, i ^ 1) for i in range(cols_n)], None, (0, True)))
        elif phase <= depth:
            due = swapped(phase)
            keys = sorted(set(due))
            if len(keys) <= 2:
                for key in keys:
                    levels = [z for z in range(depth) if due[z] == key]
                    pairs = [(i, i ^ 1) for z in levels for i in range(z * LINES, (z + 1) * LINES)]
                    steps = tuple(
                        (-key[1] if key[0] == "up" else key[1]) if z in levels else depth for z in range(depth)
                    )
                    work.append((chunk[key], pairs, None, (steps, True)))
            else:
                x = chunk[due[0]]
                for key in keys:
                    if key != due[0]:
                        levels = [level == z for z in range(depth) if due[z] == key]
                        x = jnp.where(functools.reduce(jnp.logical_or, levels), chunk[key], x)
                steps = tuple(-t if d == "up" else t for d, t in due)
                work.append((x, [(i, i ^ 1) for i in range(cols_n)], None, (steps, True)))
        else:
            gathered_all = [got for got, w in zip(done, last) if not isinstance(w[2], int)]
            shifted_first = [got for got, w in zip(done, last) if isinstance(w[2], int)]
        for k in reversed(range(1, cols_n)):
            pairs = shift_pairs(k, phase)
            if pairs:
                work.append((shifted[k - 1], pairs, k, pairs))
        before = done
        values = after([w[0] for w in work], done) if done else [w[0] for w in work]
        done = [lax.ppermute(x, "pcol", w[1]) for x, w in zip(values, work)]
        for got, (_, _, key, origin) in zip(done, work):
            if isinstance(key, int):
                arrived.append(got)
                arrived_from.append((key, origin))
            else:
                parts.append(got)
                origins.append(origin)
                if key is not None:
                    chunk[key] = got
        step = 1 << (phase - 1)
        if step < cols_n:
            if phase > 1:
                near = after([near], before)[0]
            got = lax.ppermute(near, "pcol", [(i, i ^ step) for i in range(cols_n)])
            near = jnp.concatenate([near, got])
            done = done + [got]
        if phase == 1:
            done = done + [source_rows, targets, far, chain]
    most = jnp.max(near[:, cols_n * base + excess_max])

    def gather_rest():
        mine = meta[cols_n * base + 1 : cols_n * base + excess_max]
        slot = jnp.sum(
            jnp.where(mine[:, None] == ids[None, :], jnp.arange(slots, dtype=jnp.int32)[None, :], 0), axis=1
        )
        rest = jnp.stack(
            [lax.dynamic_index_in_dim(tiles, slot[e], 0, False) for e in range(excess_max - 1)]
        )
        others = [
            lax.ppermute(rest, "pcol", [(i, i ^ k) for i in range(cols_n)]) for k in range(1, cols_n)
        ]
        return jnp.concatenate([rest] + others)

    def no_rest():
        return unwritten((cols_n * (excess_max - 1),) + tiles.shape[1:])

    rest = lax.cond(most > 1, gather_rest, no_rest)

    late_rows = after([source_rows], gathered_all)[0]
    held_p, keep_p, send_p, top_p = extract(
        parts, origins, rest, near, ids, late_rows, me, odd, cols_n, base
    )
    new_p, old_p, crossed = exchange(keep_p, send_p, top_p, far, my_row, rows_n, shifted_first)
    high, low, lower_top = panel_factors(held_p, new_p, old_p, inverses, targets, chain, me_row, group)

    late_rows = after([source_rows], [crossed])[0]
    held, keep, send, top = extract(
        parts, origins, rest, near, ids, late_rows, me, odd, cols_n, base, tiles, arrived, arrived_from
    )
    new, old, _ = exchange(keep, send, top, far, my_row, rows_n, meanwhile=high)
    return update(held, new, old, high, low, lower_top, targets, chain, me_row, me, rows_n, group)


def solution(mesh):
    in_specs = (P("prow", "pcol", None, None, None), P("prow", "pcol"), P(), P())
    out_specs = P(None, "prow", "pcol")
    return jax.shard_map(
        per_device, mesh=mesh, in_specs=in_specs, out_specs=out_specs, check_vma=False
    )
```
